256 devices in a mesh: ctx: 16 (over x_lo, y, core), vocab: 16 (over z, x_hi).
Axes of the slice: x: 4 (x_hi: 2, x_lo: 2; x = x_hi * 2 + x_lo), y: 4, z: 8, core: 2. Of those that a mesh axis runs over, the one named last changes fastest.
Arguments:
- query_rows: bfloat16 [8192, 4096], P('ctx', 'vocab'), may hold values from -6 to 6
- key_rows: bfloat16 [8192, 4096], P('ctx', 'vocab'), may hold values from -6 to 6
- value_rows: bfloat16 [8192, 4096], P('ctx', 'vocab'), may hold values from -6 to 6
- log_decay: float32 [32, 8192], P('vocab', 'ctx'), may hold values from -0.75 to 0
- segment_ids: int32 [8192], P('ctx'), may hold values from 0 to 3, as said below
- residual: bfloat16 [8192, 6144], P(('ctx', 'vocab')), may hold values from -20 to 20
- out_weight: bfloat16 [4096, 6144], P('vocab'), may hold values from -0.09375 to 0.09375
- final_gain: float32 [6144], replicated, may hold values from 0.1 to 1.9
- head_weight: bfloat16 [6144, 10240], P(None, 'vocab'), may hold values from -25 to 25
- targets: int32 [8192], P('ctx'), may hold values from 0 to 10239
Outputs:
- log_probs: float32 [8192], P(('ctx', 'vocab'))
The draws below stay inside these ranges and needn't reach their ends.
Inputs may be any that keep to these rules, and one draw needn't show every extreme that they name: `segment_ids`: never falls; each of the 4 rollouts holds 1 to 4096 tokens, one exactly 4096.
All inputs are finite; a program needn't handle non-finite values.
Results may differ from the reference program's by a relative error of at most 0.02.
Values may be sent and summed in bfloat16 or wider, within the bound.
A program may use at most 128 MiB of HBM per device.

```python
import math
import jax
import jax.numpy as jnp
from jax import lax

D = 6144
HD = 128
SPLIT_ATTN_GROUPS = 32
VOCAB_DEV = 640
TOK_CTX = 512
SEGS = 4
SEQUENCE_LENGTH = 8192
VOCAB = 10240
SPAN = 4096
N_CTX = 16
N_VOCAB = 16


def draw_log_decay(key, part):
    key = jax.random.fold_in(key, 5)
    number_of_segments = jax.random.split(key, 7)
    fast_share = 0.5
    is_fast = jax.random.uniform(number_of_segments[0], (SPLIT_ATTN_GROUPS, 1)) < fast_share
    fast_rate = jnp.exp(jax.random.uniform(number_of_segments[1], (SPLIT_ATTN_GROUPS, 1), minval=math.log(1.0 / 50.0), maxval=math.log(1.0 / 30.0)))
    slow_rate = jnp.exp(jax.random.uniform(number_of_segments[2], (SPLIT_ATTN_GROUPS, 1), minval=math.log(0.02), maxval=math.log(0.1))) * (math.log(10.0) / SEQUENCE_LENGTH)
    resting_decay_level = jnp.where(is_fast, fast_rate, slow_rate)
    tile_scaling_factor = jnp.exp(jax.random.uniform(number_of_segments[3], (SPLIT_ATTN_GROUPS, SEQUENCE_LENGTH // TOK_CTX, 1), minval=-math.log(2.0), maxval=math.log(2.0)))
    tile_scaling_factor = jnp.broadcast_to(tile_scaling_factor, (SPLIT_ATTN_GROUPS, SEQUENCE_LENGTH // TOK_CTX, TOK_CTX)).reshape(SPLIT_ATTN_GROUPS, SEQUENCE_LENGTH)
    gaussian_perturbation = jax.random.uniform(number_of_segments[4], (SPLIT_ATTN_GROUPS, SEQUENCE_LENGTH), minval=0.5, maxval=1.5)
    spike_location_index = jax.random.randint(number_of_segments[5], (SPLIT_ATTN_GROUPS, 2, 1), 0, SEQUENCE_LENGTH)
    sequence_location = jnp.arange(SEQUENCE_LENGTH)[None, None, :]
    spike_enabled_flag = jnp.any(spike_location_index == sequence_location, axis=1)
    spike_strength_level = jnp.log(jax.random.uniform(number_of_segments[6], (SPLIT_ATTN_GROUPS, SEQUENCE_LENGTH), minval=0.5, maxval=0.8))
    element_of_values_matrix = jnp.where(spike_enabled_flag, spike_strength_level, -resting_decay_level * tile_scaling_factor * gaussian_perturbation)
    return element_of_values_matrix.astype(jnp.float32)


def draw_segment_ids(key, part):
    key = jax.random.fold_in(key, 11)
    split_keys = jax.random.split(key, 2)
    long_slot = jax.random.randint(split_keys[0], (), 0, SEGS)
    remaining = SEQUENCE_LENGTH - SPAN
    cut_points = jnp.sort(jax.random.choice(split_keys[1], remaining - 1, (SEGS - 2,), replace=False).astype(jnp.int32) + 1)
    edges = jnp.concatenate([jnp.zeros((1,), jnp.int32), cut_points, jnp.full((1,), remaining, jnp.int32)])
    others = edges[1:] - edges[:-1]
    slot_index = jnp.arange(SEGS)
    other_index = jnp.clip(slot_index - (slot_index > long_slot).astype(jnp.int32), 0, SEGS - 2)
    lengths = jnp.where(slot_index == long_slot, SPAN, others[other_index])
    ends = jnp.cumsum(lengths)
    positions = jnp.arange(SEQUENCE_LENGTH)
    return jnp.sum((positions[:, None] >= ends[None, :-1]).astype(jnp.int32), axis=1).astype(jnp.int32)


def draw_residual(key, part):
    key = jax.random.fold_in(key, 7)
    number_of_segments = jax.random.split(key, 3)
    row_scale = jnp.exp(jax.random.uniform(number_of_segments[1], (SEQUENCE_LENGTH, 1), minval=-1.15, maxval=1.15))
    column_scale = jnp.exp(jax.random.uniform(number_of_segments[2], (1, D), minval=-1.15, maxval=1.15))
    base = jax.random.normal(number_of_segments[0], (SEQUENCE_LENGTH, D))
    element_of_values_matrix = base * row_scale * column_scale * 0.5
    return jnp.clip(element_of_values_matrix, -20.0, 20.0).astype(jnp.bfloat16)


def draw_head_weight(key, part):
    key = jax.random.fold_in(key, 9)
    number_of_segments = jax.random.split(key, 5)
    column_factor = jnp.exp(jax.random.uniform(number_of_segments[1], (1, VOCAB), minval=0.0, maxval=math.log(2.0)))
    slice_active = jnp.exp(jax.random.uniform(number_of_segments[4], (VOCAB // VOCAB_DEV, 1), minval=0.0, maxval=math.log(VOCAB_DEV)))
    slice_active = jnp.broadcast_to(slice_active, (VOCAB // VOCAB_DEV, VOCAB_DEV)).reshape(1, VOCAB)
    within_slice = (jnp.arange(VOCAB) % VOCAB_DEV).astype(jnp.float32)[None, :]
    column_scale = jnp.where(within_slice < slice_active, 2.5 * column_factor, 0.05)
    element_of_values_matrix = jax.random.normal(number_of_segments[0], (D, VOCAB)) * D ** (-0.5) * column_scale
    return jnp.clip(element_of_values_matrix, -25.0, 25.0).astype(jnp.bfloat16)


def place_ends(values, own_key, smallest, high):
    dims = values.shape
    place = [jax.random.randint(jax.random.fold_in(own_key, axis), (), 0, dims[axis]) for axis in range(len(dims))]
    values = values.at[tuple(place)].set(smallest)
    longest = dims.index(max(dims))
    place[longest] = (place[longest] + 1) % dims[longest]
    return values.at[tuple(place)].set(high)


def steps_of(own_key, dims, cuts, low, largest):
    def one(dim, shards_of):
        steps = jax.random.uniform(jax.random.fold_in(jax.random.fold_in(own_key, 6), dim), (shards_of,), jnp.float32, low / len(cuts), largest / len(cuts))
        return jnp.repeat(jnp.exp(steps), dims[dim] // shards_of).reshape((-1,) + (1,) * (len(dims) - dim - 1))

    loudness = one(*cuts[0])
    for cut in cuts[1:]:
        loudness = loudness * one(*cut)
    return loudness


def gaussian(key, extent, scale, reach, pieces=(), held_as=jnp.bfloat16):
    values = scale * jax.random.normal(key, extent, jnp.float32)
    if pieces:
        values = values * steps_of(key, extent, pieces, -0.22, 0.18)
    return jnp.clip(values, -reach, reach).astype(held_as)


def setup_inputs(seed: int = 0) -> dict:
    splits = jax.random.split(jax.random.key(seed), 11)
    query_rows = gaussian(splits[0], (SEQUENCE_LENGTH, SPLIT_ATTN_GROUPS * HD), 1.0, 6.0, ((0, 16), (1, 16)))
    key_rows = gaussian(splits[1], (SEQUENCE_LENGTH, SPLIT_ATTN_GROUPS * HD), 1.0, 6.0, ((0, 16), (1, 16)))
    value_rows = gaussian(splits[2], (SEQUENCE_LENGTH, SPLIT_ATTN_GROUPS * HD), 1.0, 6.0, ((0, 16), (1, 16)))
    log_decay = draw_log_decay(jax.random.fold_in(splits[10], 71), 0)
    segment_ids = draw_segment_ids(jax.random.fold_in(splits[10], 71), 0)
    residual = draw_residual(jax.random.fold_in(splits[10], 71), 0)
    out_weight = gaussian(splits[6], (SPLIT_ATTN_GROUPS * HD, D), (SPLIT_ATTN_GROUPS * HD) ** -0.5, 0.09375, ((0, 16),))
    final_gain = jnp.clip(1.0 + 0.18 * jax.random.normal(splits[7], (D,), jnp.float32), 0.1, 1.9)
    head_weight = draw_head_weight(jax.random.fold_in(splits[10], 71), 0)
    targets = place_ends(jax.random.randint(splits[9], (SEQUENCE_LENGTH,), 0, VOCAB), jax.random.fold_in(splits[9], 1), 0, VOCAB - 1).astype(jnp.int32)
    return dict(query_rows=query_rows, key_rows=key_rows, value_rows=value_rows, log_decay=log_decay, segment_ids=segment_ids, residual=residual, out_weight=out_weight, final_gain=final_gain, head_weight=head_weight, targets=targets)


EPSILON = 1e-06

def block_terms(query_heads, key_heads, value_heads, log_rates, seg_ids, prior_last):
    row_count = seg_ids.shape[0]
    cumulative = jnp.cumsum(log_rates, axis=1)
    sequence_location = jnp.arange(row_count)
    allowed = (sequence_location[:, None] >= sequence_location[None, :]) & (seg_ids[:, None] == seg_ids[None, :])
    spread = cumulative[:, :, None] - cumulative[:, None, :]
    weights = jnp.exp(jnp.where(allowed[None], spread, -jnp.inf))
    scores = jnp.einsum('rhd,shd->hrs', query_heads.astype(jnp.float32), key_heads.astype(jnp.float32))
    mixing = lax.optimization_barrier((scores * weights).astype(jnp.bfloat16))
    within = jnp.einsum('hrs,shd->hrd', mixing.astype(jnp.float32), value_heads.astype(jnp.float32))
    continues = (seg_ids == prior_last).astype(jnp.float32)
    carry_scale = jnp.exp(cumulative) * continues[None, :]
    tail_weight = jnp.exp(cumulative[:, -1:] - cumulative) * (seg_ids == seg_ids[-1]).astype(jnp.float32)[None, :]
    weighted = (key_heads.astype(jnp.float32) * tail_weight.T[:, :, None]).astype(jnp.bfloat16)
    weighted = lax.optimization_barrier(weighted)
    summary = jnp.einsum('rhd,rhe->hde', weighted.astype(jnp.float32), value_heads.astype(jnp.float32))
    passing = jnp.exp(cumulative[:, -1]) * continues[-1]
    return (within, carry_scale, passing, summary)

def finish_heads(query_heads, within, carry_scale, incoming):
    rounded = lax.optimization_barrier(incoming.astype(jnp.bfloat16))
    carried = jnp.einsum('rhd,hde->hre', query_heads.astype(jnp.float32), rounded.astype(jnp.float32))
    output = within + carry_scale[:, :, None] * carried
    scaled = output * lax.rsqrt(lax.optimization_barrier(jnp.mean(output * output, axis=-1, keepdims=True)) + EPSILON)
    return jnp.transpose(scaled, (1, 0, 2)).reshape(query_heads.shape[0], -1).astype(jnp.bfloat16)

def reference(query_rows, key_rows, value_rows, log_decay, segment_ids, residual, out_weight, final_gain, head_weight, targets):
    query_blocks = query_rows.reshape(N_CTX, TOK_CTX, SPLIT_ATTN_GROUPS, HD)
    key_blocks = key_rows.reshape(N_CTX, TOK_CTX, SPLIT_ATTN_GROUPS, HD)
    value_blocks = value_rows.reshape(N_CTX, TOK_CTX, SPLIT_ATTN_GROUPS, HD)
    rate_blocks = jnp.transpose(log_decay.reshape(SPLIT_ATTN_GROUPS, N_CTX, TOK_CTX), (1, 0, 2))
    segment_blocks = segment_ids.reshape(N_CTX, TOK_CTX)

    def advance(carried, inputs):
        incoming, prior_last = carried
        query_heads, key_heads, value_heads, log_rates, seg_ids = inputs
        within, carry_scale, passing, summary = block_terms(query_heads, key_heads, value_heads, log_rates, seg_ids, prior_last)
        attention = finish_heads(query_heads, within, carry_scale, incoming)
        return ((passing[:, None, None] * incoming + summary, seg_ids[-1]), attention)
    start_state = (jnp.zeros((SPLIT_ATTN_GROUPS, HD, HD), jnp.float32), jnp.zeros((), jnp.int32))
    finished, attention = lax.scan(advance, start_state, (query_blocks, key_blocks, value_blocks, rate_blocks, segment_blocks))
    attention = attention.reshape(SEQUENCE_LENGTH, SPLIT_ATTN_GROUPS * HD)
    group_width = SPLIT_ATTN_GROUPS * HD // N_VOCAB

    def add_group(member, running):
        offset = (member * group_width).astype(jnp.int32)
        columns = lax.dynamic_slice_in_dim(attention, offset, group_width, 1)
        weight_rows = lax.dynamic_slice_in_dim(out_weight, offset, group_width, 0)
        term = jnp.dot(columns, weight_rows, preferred_element_type=jnp.float32).astype(jnp.bfloat16)
        term = lax.optimization_barrier(term)
        return running + term.astype(jnp.float32)
    summed = lax.fori_loop(jnp.int32(0), jnp.int32(N_VOCAB), add_group, jnp.zeros((SEQUENCE_LENGTH, D), jnp.float32))

    def score_block(inputs):
        block_sum, block_residual, block_targets = inputs
        hidden = block_residual.astype(jnp.float32) + block_sum
        normed = (hidden * lax.rsqrt(lax.optimization_barrier(jnp.mean(hidden * hidden, axis=1, keepdims=True)) + EPSILON) * final_gain).astype(jnp.bfloat16)
        logits = jnp.dot(normed, head_weight, preferred_element_type=jnp.float32)
        picked = jnp.take_along_axis(logits, block_targets[:, None], axis=1)[:, 0]
        return picked - jax.nn.logsumexp(logits, axis=1)
    result = lax.map(score_block, (summed.reshape(N_CTX, TOK_CTX, D), residual.reshape(N_CTX, TOK_CTX, D), targets.reshape(N_CTX, TOK_CTX)))
    return result.reshape(SEQUENCE_LENGTH)
```

```python
import jax
import jax.numpy as jnp
from jax import lax
from jax.experimental import pallas as pl
from jax.experimental.pallas import tpu as pltpu
from jax.sharding import PartitionSpec as P

EPSILON = 1e-06
MESH = pl.DeviceIdType.MESH
F32 = jnp.float32
BF16 = jnp.bfloat16

TOK = 512
D = 6144
HD = 128
NV = 640
CH = 32
SUB = 1536
NZ = 8
TILE = 256

SLOT_OFFSET = (0, -1, 1, -2, 2, -3, 3, 4)
GATHER_FROM = ((0, 1, 3, 5), (0, 2, 4, 6))
GATHER_TO = ((1, 3, 5, 7), (2, 4, 6, 7))
SUB_ORDER = ((0, 1, 2, 3), (2, 3, 0, 1))
SUM_SLOTS = ((4, 3, 2, 1), (4, 5, 6, 7))

WO_PIECES = 2
WH_PIECES = 4
WO_PART = 32
WH_PART = 192


def dot(a, b):
    return jnp.dot(a, b, preferred_element_type=F32)


def kernel(
    q_ref, k_ref, v_ref, ld_ref, seg_ref, tgt_ref, res_ref, gain_ref, wo_ref, wh_ref,
    out_ref,
    wo, wh, part, stage, landed, gathered, logits, hidden, within, columns, goals,
    attn, attn_in, lhs, state_out, state_in, stats, stats_in,
    local_sem, piece_send, piece_recv, state_send, state_recv, attn_send, attn_recv,
    sum_send, sum_recv, gather_send, gather_recv, stats_send, stats_recv,
):
    ctx = lax.axis_index("ctx")
    vocab = lax.axis_index("vocab")
    x_lo = ctx // 8
    y = lax.rem(ctx // 2, 4)
    core = lax.rem(ctx, 2)
    z = vocab // 2
    x_hi = lax.rem(vocab, 2)

    def at_y(by):
        return x_lo * 8 + lax.rem(y + by + 4, 4) * 2 + core

    def at_z(by):
        return lax.rem(z + by + NZ, NZ) * 2 + x_hi

    sibling = (ctx + 1 - 2 * core, vocab)
    y_peer = {by: (at_y(by), vocab) for by in (-1, 1, 2)}
    lo_peer = (lax.rem(ctx + 8, 16), vocab)
    cut_peer = (lax.rem(ctx + 8, 16), z * 2 + 1 - x_hi)
    hi_peer = (ctx, z * 2 + 1 - x_hi)
    z_peer = {by: (ctx, at_z(by)) for by in (-3, -2, -1, 1, 2, 3, 4)}

    barrier = pltpu.get_barrier_semaphore()
    peers = [sibling, lo_peer, cut_peer, hi_peer, *y_peer.values(), *z_peer.values()]
    for peer in peers:
        pl.semaphore_signal(barrier, inc=1, device_id=peer, device_id_type=MESH)

    own_wo = pltpu.make_async_copy(wo_ref, wo.at[pl.ds(0, 256)], local_sem.at[0])
    own_wh = pltpu.make_async_copy(wh_ref, wh.at[:, pl.ds(0, NV)], local_sem.at[1])
    own_wo.start()

    waiting = []

    def send(src, dst, send_sem, recv_sem, peer):
        copy = pltpu.make_async_remote_copy(
            src_ref=src, dst_ref=dst, send_sem=send_sem, recv_sem=recv_sem,
            device_id=peer, device_id_type=MESH,
        )
        copy.start()
        waiting.append(copy)
        return copy

    def rows_of(piece, by, of_core, size):
        index = lax.rem(y + by + 4, 4) * 2 + of_core
        if piece < WO_PIECES:
            return pl.multiple_of(index * WO_PART, WO_PART)
        base = (piece - WO_PIECES) * 8 * WH_PART
        return pl.multiple_of(base + index * WH_PART, WH_PART)

    def piece_view(piece, by, low, size):
        start = rows_of(piece, by, core, size) + low
        if piece < WO_PIECES:
            return wo.at[pl.ds(256 + pl.multiple_of(start, 16), size), pl.ds(piece * 3072, 3072)]
        return wh.at[pl.ds(pl.multiple_of(start, 16), size), pl.ds(NV, NV)]

    def piece_source(piece):
        if piece < WO_PIECES:
            rows = pl.ds(rows_of(piece, 0, core, WO_PART), WO_PART)
            return wo_ref.at[rows, pl.ds(piece * 3072, 3072)]
        return wh_ref.at[pl.ds(rows_of(piece, 0, core, WH_PART), WH_PART), :]

    moves = [dict() for _ in range(WO_PIECES + WH_PIECES)]

    def piece_send_to(piece, name, index, src, dst, peer):
        moves[piece][name] = send(
            src, dst, piece_send.at[piece, index], piece_recv.at[piece, index], peer
        )

    def part_size(piece):
        return WO_PART if piece < WO_PIECES else WH_PART

    def fetch_0(piece):
        view = piece_view(piece, 0, 0, part_size(piece))
        piece_send_to(piece, "cut", 0, piece_source(piece), view, cut_peer)

    def fetch_1(piece):
        moves[piece]["cut"].wait_recv()
        view = piece_view(piece, 0, 0, part_size(piece))
        piece_send_to(piece, "up", 1, view, view, y_peer[1])
        piece_send_to(piece, "down", 2, view, view, y_peer[-1])
        piece_send_to(piece, "core0", 5, view, view, sibling)

    def fetch_2(piece):
        size = part_size(piece)
        half = size // 2
        moves[piece]["up"].wait_recv()
        view = piece_view(piece, -1, 0, half)
        piece_send_to(piece, "up2", 3, view, view, y_peer[1])
        view = piece_view(piece, -1, 0, size)
        piece_send_to(piece, "core1", 6, view, view, sibling)
        moves[piece]["down"].wait_recv()
        view = piece_view(piece, 1, half, half)
        piece_send_to(piece, "down2", 4, view, view, y_peer[-1])
        view = piece_view(piece, 1, 0, size)
        piece_send_to(piece, "core2", 7, view, view, sibling)

    def fetch_3(piece):
        moves[piece]["up2"].wait_recv()
        moves[piece]["down2"].wait_recv()
        view = piece_view(piece, 2, 0, part_size(piece))
        piece_send_to(piece, "core3", 8, view, view, sibling)

    def fetch_4(piece):
        for name in ("core0", "core1", "core2", "core3"):
            moves[piece][name].wait_recv()

    lane = lax.broadcasted_iota(jnp.int32, (8, TOK), 1)
    running = jnp.concatenate([ld_ref[...], jnp.zeros((6, TOK), F32)], axis=0)
    shift = 1
    while shift < TOK:
        running = running + jnp.where(lane >= shift, pltpu.roll(running, shift, axis=1), 0.0)
        shift *= 2
    seg_row = seg_ref[...].astype(F32)
    table = jnp.concatenate(
        [running[0:2], seg_row, tgt_ref[...].astype(F32), jnp.zeros((124, TOK), F32)], axis=0
    )
    columns[...] = table.T
    seg_col = columns[:, 2:3]
    seg_last = seg_col[TOK - 1 : TOK, :]

    decay = []
    own_state = []
    for h in range(2):
        head = slice(h * HD, (h + 1) * HD)
        cum_col = columns[:, h : h + 1]
        last = cum_col[TOK - 1 : TOK, :]
        tail = jnp.where(seg_col == seg_last, jnp.exp(last - cum_col), 0.0)
        weighted = (k_ref[:, head].astype(F32) * tail).astype(BF16)
        summary = lax.dot_general(
            weighted, v_ref[:, head], (((0,), (0,)), ((), ())), preferred_element_type=F32
        )
        own_state.append(summary)
        decay.append(jnp.exp(last))

    def pack(slot, states, decays, seg):
        for h in range(2):
            state_out[slot, h * HD : (h + 1) * HD, :] = states[h].astype(BF16)
        row = lax.broadcasted_iota(jnp.int32, (16, HD), 0)
        tops = [d.astype(BF16).astype(F32) for d in decays]
        block = jnp.where(row == 0, tops[0], 0.0)
        block = jnp.where(row == 1, decays[0] - tops[0], block)
        block = jnp.where(row == 2, tops[1], block)
        block = jnp.where(row == 3, decays[1] - tops[1], block)
        block = jnp.where(row == 4, seg, block)
        state_out[slot, 2 * HD : 2 * HD + 16, :] = block.astype(BF16)

    def unpack(buffer, slot):
        states = [buffer[slot, h * HD : (h + 1) * HD, :].astype(F32) for h in range(2)]
        block = buffer[slot, 2 * HD : 2 * HD + 16, :].astype(F32)
        decays = [block[0:1, 0:1] + block[1:2, 0:1], block[2:3, 0:1] + block[3:4, 0:1]]
        return states, decays, block[4:5, 0:1]

    def join(first, second):
        states = [
            jnp.where(first[2] == second[2], second[1][h], 0.0) * first[0][h] + second[0][h]
            for h in range(2)
        ]
        return states, [first[1][h] * second[1][h] for h in range(2)], second[2]

    def choose(flag, a, b):
        return (
            [jnp.where(flag, a[0][h], b[0][h]) for h in range(2)],
            [jnp.where(flag, a[1][h], b[1][h]) for h in range(2)],
            jnp.where(flag, a[2], b[2]),
        )

    pack(0, own_state, decay, seg_last)
    pl.semaphore_wait(barrier, len(peers))
    to_core = send(state_out.at[0], state_in.at[0], state_send.at[0], state_recv.at[0], sibling)
    for piece in range(WO_PIECES):
        fetch_0(piece)

    def inside(h):
        head = slice(h * HD, (h + 1) * HD)
        cum_col = columns[:, h : h + 1]
        cum_row = running[h : h + 1, :]
        for low in (0, 256):
            high = low + 256
            scores = lax.dot_general(
                q_ref[low:high, head], k_ref[0:high, head], (((1,), (1,)), ((), ())),
                preferred_element_type=F32,
            )
            at_row = lax.broadcasted_iota(jnp.int32, (256, high), 0) + low
            at_col = lax.broadcasted_iota(jnp.int32, (256, high), 1)
            allowed = (at_row >= at_col) & (seg_col[low:high] == seg_row[:, 0:high])
            spread = cum_col[low:high] - cum_row[:, 0:high]
            weights = jnp.exp(jnp.where(allowed, spread, -1e30))
            mixing = (scores * weights).astype(BF16)
            within[h, low:high, :] = dot(mixing, v_ref[0:high, head])

    to_core.wait_recv()
    own = unpack(state_out, 0)
    own = (own_state, decay, seg_last)
    other = unpack(state_in, 0)
    first = choose(core == 0, own, other)
    second = choose(core == 0, other, own)
    chip = join(first, second)
    pack(1, *chip)
    to_y = []
    for index, by in enumerate((-1, 1, 2)):
        to_y.append(
            send(
                state_out.at[1], state_in.at[1 + index], state_send.at[1 + index],
                state_recv.at[1 + index], y_peer[by],
            )
        )
    own_wh.start()
    inside(0)
    for copy in to_y:
        copy.wait_recv()
    chips = {0: chip}
    for index, by in enumerate((1, -1, 2)):
        chips[by] = unpack(state_in, 1 + index)

    def chip_at(target):
        picked = chips[0]
        for by in (1, -1, 2):
            picked = choose(lax.rem(y + by + 4, 4) == target, chips[by], picked)
        return picked

    nothing = ([jnp.zeros((HD, HD), F32)] * 2, [jnp.ones((1, 1), F32)] * 2, jnp.zeros((1, 1), F32))
    total = chip_at(0)
    before = choose(y == 0, nothing, total)
    for target in range(1, 4):
        total = join(total, chip_at(target))
        before = choose(y > target, total, before)
    pack(2, *total)
    to_lo = send(state_out.at[2], state_in.at[4], state_send.at[4], state_recv.at[4], lo_peer)
    for piece in range(WO_PIECES):
        fetch_1(piece)
    inside(1)
    to_lo.wait_recv()
    earlier = unpack(state_in, 4)
    joined = choose(y == 0, earlier, join(earlier, before))
    before = choose(x_lo == 0, before, joined)
    fresh = (x_lo == 0) & (y == 0)
    with_first = choose(fresh, first, join(before, first))
    before = choose(core == 0, before, with_first)
    prior = before[2]

    sent_attn = []
    for h in range(2):
        head = slice(h * HD, (h + 1) * HD)
        scale = jnp.where(seg_col == prior, jnp.exp(columns[:, h : h + 1]), 0.0)
        carried = dot(q_ref[:, head], before[0][h].astype(BF16))
        output = within[h] + scale * carried
        mean = jnp.mean(output * output, axis=-1, keepdims=True)
        scaled = (output * lax.rsqrt(mean + EPSILON)).astype(BF16)
        for j in range(NZ):
            for half in range(2):
                low = (2 * j + half) * CH
                attn[h, half, j] = scaled[low : low + CH]
        sent_attn.append(
            send(attn.at[h, 1 - x_hi], attn_in.at[h], attn_send.at[h], attn_recv.at[h], hi_peer)
        )
    for piece in range(WO_PIECES):
        fetch_2(piece)
    for piece in range(WO_PIECES, WO_PIECES + WH_PIECES):
        fetch_0(piece)
    for d in range(NZ):
        chunk = lax.rem(z + d, NZ)
        rows = slice(d * CH, (d + 1) * CH)
        for h in range(2):
            lhs[rows, h * HD : (h + 1) * HD] = attn[h, x_hi, chunk]
    for slot, offset in enumerate(SLOT_OFFSET):
        chunk = lax.rem(z + offset + NZ, NZ)
        rows = pl.ds(pl.multiple_of((2 * chunk + x_hi) * CH, CH), CH)
        goals[slot * CH : (slot + 1) * CH, :] = columns[rows, :]
    for copy in sent_attn:
        copy.wait_recv()
    for d in range(NZ):
        chunk = lax.rem(z + d, NZ)
        rows = slice(d * CH, (d + 1) * CH)
        for h in range(2):
            lhs[rows, 256 + h * HD : 256 + (h + 1) * HD] = attn_in[h, chunk]
    for piece in range(WO_PIECES):
        fetch_3(piece)
    own_wo.wait()
    for piece in range(WO_PIECES):
        fetch_4(piece)

    def project(sub):
        def tile(t, carry):
            cols = pl.ds(pl.multiple_of(sub * SUB + t * 512, 512), 512)
            part[:, :, cols] = dot(lhs[...], wo[:, cols]).reshape(NZ, CH, 512)
            return carry

        lax.fori_loop(0, SUB // 512, tile, 0)

    sums = {}

    def sum_send_to(way, step, sub):
        cols = slice(sub * SUB, (sub + 1) * SUB)
        value = part[SUM_SLOTS[way][step], :, cols]
        if (way, step - 1, sub) in sums:
            sums[way, step - 1, sub].wait_recv()
            value = value + landed[way, step - 1, :, cols].astype(F32)
        stage[way, step, :, cols] = value.astype(BF16)
        index = (way * 4 + step) * 4 + sub
        sums[way, step, sub] = send(
            stage.at[way, step, :, pl.ds(sub * SUB, SUB)],
            landed.at[way, step, :, pl.ds(sub * SUB, SUB)],
            sum_send.at[index], sum_recv.at[index], z_peer[1 if way == 0 else -1],
        )

    for i in range(2):
        for way in range(2):
            project(SUB_ORDER[way][i])
            sum_send_to(way, 0, SUB_ORDER[way][i])
    service = [
        lambda: fetch_1(2),
        lambda: fetch_1(3),
        lambda: fetch_2(2),
        lambda: (fetch_1(4), fetch_2(3)),
        lambda: (fetch_1(5), fetch_3(2)),
        lambda: (fetch_2(4), fetch_3(3)),
        lambda: fetch_2(5),
    ]
    count = 0
    for step in range(1, 4):
        for i in (2, 3, 0, 1):
            for way in range(2):
                sum_send_to(way, step, SUB_ORDER[way][i])
            count += 1
            if count >= 5 and service:
                service.pop(0)()
    while service:
        service.pop(0)()

    square = jnp.zeros((CH, 1), F32)
    for i in (2, 0, 3, 1):
        sub = i
        cols = slice(sub * SUB, (sub + 1) * SUB)
        for way in range(2):
            sums[way, 3, sub].wait_recv()
        value = part[0, :, cols] + landed[0, 3, :, cols].astype(F32)
        value = value + landed[1, 3, :, cols].astype(F32) + res_ref[:, cols].astype(F32)
        hidden[:, cols] = value
        square = square + jnp.sum(value * value, axis=1, keepdims=True)
    scale = lax.rsqrt(square / D + EPSILON)

    gathers = {}

    def gather_to(way, step, sub):
        if step > 0:
            gathers[way, step - 1, sub].wait_recv()
        src = GATHER_FROM[way][step] * CH
        dst = GATHER_TO[way][step] * CH
        cols = pl.ds(sub * SUB, SUB)
        index = (way * 4 + step) * 4 + sub
        gathers[way, step, sub] = send(
            gathered.at[pl.ds(src, CH), cols], gathered.at[pl.ds(dst, CH), cols],
            gather_send.at[index], gather_recv.at[index], z_peer[1 if way == 0 else -1],
        )

    for sub in (0, 2, 1, 3):
        cols = slice(sub * SUB, (sub + 1) * SUB)
        gathered[0:CH, cols] = (hidden[:, cols] * scale * gain_ref[:, cols]).astype(BF16)
        for way in range(2):
            gather_to(way, 0, sub)

    own_wh.wait()
    own_offset = vocab * NV
    other_offset = (z * 2 + 1 - x_hi) * NV

    def multiply(first, count, tile):
        rows = slice(first * CH, (first + count) * CH)
        cols = slice(tile * TILE, (tile + 1) * TILE)
        logits[rows, cols] = dot(gathered[rows, :], wh[:, cols])

    def summarize(first, count):
        size = count * CH
        rows = slice(first * CH, (first + count) * CH)
        values = logits[rows, :]
        top = jnp.max(values, axis=1, keepdims=True)
        mass = jnp.sum(jnp.exp(values - top), axis=1, keepdims=True)
        column = lax.broadcasted_iota(jnp.int32, (size, 2 * NV), 1)
        column = jnp.where(column < NV, column + own_offset, column - NV + other_offset)
        goal = goals[rows, 3:4].astype(jnp.int32)
        hit = jnp.sum(jnp.where(column == goal, values, 0.0), axis=1, keepdims=True)
        place = lax.broadcasted_iota(jnp.int32, (size, HD), 1)
        block = jnp.where(place == 0, top, jnp.where(place == 1, mass, hit))
        stats[rows, :] = block
        for slot in range(first, first + count):
            if slot > 0:
                stats_moves[slot] = send(
                    stats.at[pl.ds(slot * CH, CH)], stats_in.at[slot],
                    stats_send.at[slot], stats_recv.at[slot], z_peer[SLOT_OFFSET[slot]],
                )

    stats_moves = {}
    fetch_3(4)
    fetch_3(5)
    for i in range(4):
        for way in range(2):
            gather_to(way, 1, SUB_ORDER[way][i])
    for piece in range(WO_PIECES, WO_PIECES + WH_PIECES):
        fetch_4(piece)
    for i in range(4):
        multiply(0, 3, i)
        for way in range(2):
            gather_to(way, 2, SUB_ORDER[way][i])
    multiply(0, 3, 4)
    summarize(0, 3)
    for i in range(2):
        multiply(3, 2, i)
        for way in range(2):
            gather_to(way, 3, SUB_ORDER[way][i])
    for i in range(2, 5):
        multiply(3, 2, i)
    summarize(3, 2)
    for way in range(2):
        for i in range(2, 4):
            gathers[way, 2, SUB_ORDER[way][i]].wait_recv()
        for i in range(2):
            gathers[way, 3, SUB_ORDER[way][i]].wait_recv()
    for i in range(5):
        multiply(5, 3, i)
    summarize(5, 3)

    blocks = [stats[0:CH, :]]
    for slot in range(1, NZ):
        stats_moves[slot].wait_recv()
        blocks.append(stats_in[slot])
    top = blocks[0][:, 0:1]
    for block in blocks[1:]:
        top = jnp.maximum(top, block[:, 0:1])
    mass = jnp.zeros((CH, 1), F32)
    hit = jnp.zeros((CH, 1), F32)
    for block in blocks:
        mass = mass + block[:, 1:2] * jnp.exp(block[:, 0:1] - top)
        hit = hit + block[:, 2:3]
    result = jnp.broadcast_to(hit - top - jnp.log(mass), (CH, HD))
    padded = jnp.concatenate([result, jnp.zeros((HD - CH, HD), F32)], axis=0)
    out_ref[...] = padded.T[0:1, 0:CH]
    for copy in waiting:
        copy.wait_send()


def shards(
    query_rows, key_rows, value_rows, log_decay, segment_ids, residual, out_weight, final_gain,
    head_weight, targets,
):
    vmem = pl.BlockSpec(memory_space=pltpu.VMEM)
    hbm = pl.BlockSpec(memory_space=pl.ANY)
    dma = pltpu.SemaphoreType.DMA
    pieces = WO_PIECES + WH_PIECES
    result = pl.pallas_call(
        kernel,
        out_shape=jax.ShapeDtypeStruct((1, CH), F32),
        in_specs=[vmem] * 8 + [hbm] * 2,
        out_specs=vmem,
        scratch_shapes=[
            pltpu.VMEM((512, D), BF16),
            pltpu.VMEM((D, 2 * NV), BF16),
            pltpu.VMEM((NZ, CH, D), F32),
            pltpu.VMEM((2, 4, CH, D), BF16),
            pltpu.VMEM((2, 4, CH, D), BF16),
            pltpu.VMEM((NZ * CH, D), BF16),
            pltpu.VMEM((NZ * CH, 2 * NV), F32),
            pltpu.VMEM((CH, D), F32),
            pltpu.VMEM((2, TOK, HD), F32),
            pltpu.VMEM((TOK, HD), F32),
            pltpu.VMEM((NZ * CH, HD), F32),
            pltpu.VMEM((2, 2, NZ, CH, HD), BF16),
            pltpu.VMEM((2, NZ, CH, HD), BF16),
            pltpu.VMEM((NZ * CH, 512), BF16),
            pltpu.VMEM((3, 2 * HD + 16, HD), BF16),
            pltpu.VMEM((5, 2 * HD + 16, HD), BF16),
            pltpu.VMEM((NZ * CH, HD), F32),
            pltpu.VMEM((NZ, CH, HD), F32),
            dma((2,)),
            dma((pieces, 9)),
            dma((pieces, 9)),
            dma((5,)),
            dma((5,)),
            dma((2,)),
            dma((2,)),
            dma((32,)),
            dma((32,)),
            dma((32,)),
            dma((32,)),
            dma((NZ,)),
            dma((NZ,)),
        ],
        compiler_params=pltpu.CompilerParams(
            collective_id=0, has_side_effects=True, vmem_limit_bytes=56 * 1024 * 1024
        ),
        name="layer",
    )(
        query_rows, key_rows, value_rows, log_decay, segment_ids.reshape(1, -1),
        targets.reshape(1, -1), residual, final_gain.reshape(1, -1), out_weight, head_weight,
    )
    return result.reshape(CH)


def solution(mesh):
    in_specs = (
        P("ctx", "vocab"),
        P("ctx", "vocab"),
        P("ctx", "vocab"),
        P("vocab", "ctx"),
        P("ctx"),
        P(("ctx", "vocab"), None),
        P("vocab", None),
        P(),
        P(None, "vocab"),
        P("ctx"),
    )
    out_specs = P(("ctx", "vocab"))
    return jax.shard_map(shards, mesh=mesh, in_specs=in_specs, out_specs=out_specs, check_vma=False)
```

```python
import jax
import jax.numpy as jnp
from jax import lax
from jax.experimental import pallas as pl
from jax.experimental.pallas import tpu as pltpu
from jax.sharding import PartitionSpec as P

EPSILON = 1e-06
MESH = pl.DeviceIdType.MESH
F32 = jnp.float32
BF16 = jnp.bfloat16

TOK = 512
D = 6144
HD = 128
NV = 640
CH = 32
SUB = 1536
NZ = 8
TILE = 256

SLOT_OFFSET = (0, -1, 1, -2, 2, -3, 3, 4)
GATHER_FROM = ((0, 1, 3, 5), (0, 2, 4, 6))
GATHER_TO = ((1, 3, 5, 7), (2, 4, 6, 7))
SUB_ORDER = ((0, 1, 2, 3), (2, 3, 0, 1))
SUM_SLOTS = ((4, 3, 2, 1), (4, 5, 6, 7))

WO_ORDER = (0, 2, 1, 3)
KINDS = "YYXY" "YYYYYX"
WO_PIECES = 4
WH_PIECES = 6
WO_ROWS = 256
WH_ROWS = 1024


def dot(a, b):
    return jnp.dot(a, b, preferred_element_type=F32)


def kernel(
    q_hbm, k_hbm, v_hbm, ld_hbm, seg_hbm, tgt_hbm, res_hbm, gain_hbm, wo_ref, wh_ref,
    out_ref,
    q_ref, k_ref, v_ref, ld_ref, seg_ref, tgt_ref, res_ref, gain_ref,
    wo, wh, part, stage, landed, gathered, logits, scales, within, columns, goals,
    attn, attn_in, lhs, state_out, state_in, stats, stats_in,
    local_sem, piece_send, piece_recv, state_send, state_recv, attn_send, attn_recv,
    sum_send, sum_recv, gather_send, gather_recv, scale_send, scale_recv, stats_send, stats_recv,
):
    ctx = lax.axis_index("ctx")
    vocab = lax.axis_index("vocab")
    x_lo = ctx // 8
    y = lax.rem(ctx // 2, 4)
    core = lax.rem(ctx, 2)
    z = vocab // 2
    x_hi = lax.rem(vocab, 2)

    def at_y(by):
        return x_lo * 8 + lax.rem(y + by + 4, 4) * 2 + core

    def at_z(by):
        return lax.rem(z + by + NZ, NZ) * 2 + x_hi

    sibling = (ctx + 1 - 2 * core, vocab)
    y_peer = {by: (at_y(by), vocab) for by in (-1, 1, 2)}
    lo_peer = (lax.rem(ctx + 8, 16), vocab)
    cut_peer = (lax.rem(ctx + 8, 16), z * 2 + 1 - x_hi)
    hi_peer = (ctx, z * 2 + 1 - x_hi)
    z_peer = {by: (ctx, at_z(by)) for by in (-3, -2, -1, 1, 2, 3, 4)}

    barrier = pltpu.get_barrier_semaphore()
    peers = [sibling, lo_peer, cut_peer, hi_peer, *y_peer.values(), *z_peer.values()]
    for peer in peers:
        pl.semaphore_signal(barrier, inc=1, device_id=peer, device_id_type=MESH)

    def load(index, src, dst):
        copy = pltpu.make_async_copy(src, dst, local_sem.at[index])
        copy.start()
        return copy

    small = [
        load(0, ld_hbm, ld_ref), load(1, seg_hbm, seg_ref), load(2, tgt_hbm, tgt_ref),
        load(3, k_hbm, k_ref), load(4, v_hbm, v_ref),
    ]
    load_q = load(5, q_hbm, q_ref)
    own_wo = load(6, wo_ref, wo.at[pl.ds(0, 256)])

    waiting = []

    def send(src, dst, send_sem, recv_sem, peer):
        copy = pltpu.make_async_remote_copy(
            src_ref=src, dst_ref=dst, send_sem=send_sem, recv_sem=recv_sem,
            device_id=peer, device_id_type=MESH,
        )
        copy.start()
        waiting.append(copy)
        return copy

    def part_rows(piece):
        rows = WO_ROWS if piece < WO_PIECES else WH_ROWS
        return rows // (8 if KINDS[piece] == "Y" else 4)

    def part_start(piece, by):
        size = part_rows(piece)
        if KINDS[piece] == "Y":
            start = (lax.rem(y + by + 4, 4) * 2 + core) * size
        else:
            start = (lax.rem(x_lo + by, 2) * 2 + core) * size
        if piece >= WO_PIECES:
            start = start + (piece - WO_PIECES) * WH_ROWS
        return start

    def piece_view(piece, by, low=0, size=None):
        start = part_start(piece, by) + low
        size = part_rows(piece) if size is None else size
        if piece < WO_PIECES:
            cols = pl.ds(WO_ORDER[piece] * SUB, SUB)
            return wo.at[pl.ds(WO_ROWS + pl.multiple_of(start, 16), size), cols]
        return wh.at[pl.ds(pl.multiple_of(start, 16), size), pl.ds(NV, NV)]

    def piece_source(piece):
        rows = pl.ds(pl.multiple_of(part_start_other(piece), 16), part_rows(piece))
        if piece < WO_PIECES:
            return wo_ref.at[rows, pl.ds(WO_ORDER[piece] * SUB, SUB)]
        return wh_ref.at[rows, :]

    def part_start_other(piece):
        return part_start(piece, 0 if KINDS[piece] == "Y" else 1)

    moves = [dict() for _ in range(WO_PIECES + WH_PIECES)]

    def piece_move(piece, name, index, src, dst, peer):
        moves[piece][name] = send(
            src, dst, piece_send.at[piece, index], piece_recv.at[piece, index], peer
        )

    def fetch_0(piece):
        there = piece_view(piece, 0 if KINDS[piece] == "Y" else 1)
        piece_move(piece, "cut", 0, piece_source(piece), there, cut_peer)

    def fetch_1(piece):
        moves[piece]["cut"].wait_recv()
        view = piece_view(piece, 0)
        if KINDS[piece] == "Y":
            piece_move(piece, "up", 1, view, view, y_peer[1])
            piece_move(piece, "down", 2, view, view, y_peer[-1])
        else:
            piece_move(piece, "lo", 1, view, view, lo_peer)
        piece_move(piece, "core0", 5, view, view, sibling)

    def fetch_2(piece):
        if KINDS[piece] == "X":
            moves[piece]["lo"].wait_recv()
            view = piece_view(piece, 1)
            piece_move(piece, "core1", 6, view, view, sibling)
            return
        half = part_rows(piece) // 2
        moves[piece]["up"].wait_recv()
        view = piece_view(piece, -1, 0, half)
        piece_move(piece, "up2", 3, view, view, y_peer[1])
        view = piece_view(piece, -1)
        piece_move(piece, "core1", 6, view, view, sibling)
        moves[piece]["down"].wait_recv()
        view = piece_view(piece, 1, half, half)
        piece_move(piece, "down2", 4, view, view, y_peer[-1])
        view = piece_view(piece, 1)
        piece_move(piece, "core2", 7, view, view, sibling)

    def fetch_3(piece):
        moves[piece]["up2"].wait_recv()
        moves[piece]["down2"].wait_recv()
        view = piece_view(piece, 2)
        piece_move(piece, "core3", 8, view, view, sibling)

    def fetch_4(piece):
        for name in ("core0", "core1", "core2", "core3"):
            if name in moves[piece]:
                moves[piece][name].wait_recv()

    for copy in small:
        copy.wait()
    lane = lax.broadcasted_iota(jnp.int32, (8, TOK), 1)
    running = jnp.concatenate([ld_ref[...], jnp.zeros((6, TOK), F32)], axis=0)
    shift = 1
    while shift < TOK:
        running = running + jnp.where(lane >= shift, pltpu.roll(running, shift, axis=1), 0.0)
        shift *= 2
    seg_row = seg_ref[...].astype(F32)
    table = jnp.concatenate(
        [running[0:2], seg_row, tgt_ref[...].astype(F32), jnp.zeros((124, TOK), F32)], axis=0
    )
    columns[...] = table.T
    seg_col = columns[:, 2:3]
    seg_last = seg_col[TOK - 1 : TOK, :]

    decay = []
    own_state = []
    for h in range(2):
        head = slice(h * HD, (h + 1) * HD)
        cum_col = columns[:, h : h + 1]
        last = cum_col[TOK - 1 : TOK, :]
        tail = jnp.where(seg_col == seg_last, jnp.exp(last - cum_col), 0.0)
        weighted = (k_ref[:, head].astype(F32) * tail).astype(BF16)
        summary = lax.dot_general(
            weighted, v_ref[:, head], (((0,), (0,)), ((), ())), preferred_element_type=F32
        )
        own_state.append(summary)
        decay.append(jnp.exp(last))

    def pack(slot, states, decays, seg):
        for h in range(2):
            state_out[slot, h * HD : (h + 1) * HD, :] = states[h].astype(BF16)
        row = lax.broadcasted_iota(jnp.int32, (16, HD), 0)
        tops = [d.astype(BF16).astype(F32) for d in decays]
        block = jnp.where(row == 0, tops[0], 0.0)
        block = jnp.where(row == 1, decays[0] - tops[0], block)
        block = jnp.where(row == 2, tops[1], block)
        block = jnp.where(row == 3, decays[1] - tops[1], block)
        block = jnp.where(row == 4, seg, block)
        state_out[slot, 2 * HD : 2 * HD + 16, :] = block.astype(BF16)

    def unpack(buffer, slot):
        states = [buffer[slot, h * HD : (h + 1) * HD, :].astype(F32) for h in range(2)]
        block = buffer[slot, 2 * HD : 2 * HD + 16, :].astype(F32)
        decays = [block[0:1, 0:1] + block[1:2, 0:1], block[2:3, 0:1] + block[3:4, 0:1]]
        return states, decays, block[4:5, 0:1]

    def join(first, second):
        states = [
            jnp.where(first[2] == second[2], second[1][h], 0.0) * first[0][h] + second[0][h]
            for h in range(2)
        ]
        return states, [first[1][h] * second[1][h] for h in range(2)], second[2]

    def choose(flag, a, b):
        return (
            [jnp.where(flag, a[0][h], b[0][h]) for h in range(2)],
            [jnp.where(flag, a[1][h], b[1][h]) for h in range(2)],
            jnp.where(flag, a[2], b[2]),
        )

    pack(0, own_state, decay, seg_last)
    pl.semaphore_wait(barrier, len(peers))
    to_core = send(state_out.at[0], state_in.at[0], state_send.at[0], state_recv.at[0], sibling)
    for piece in range(WO_PIECES):
        fetch_0(piece)

    def inside(h):
        head = slice(h * HD, (h + 1) * HD)
        cum_col = columns[:, h : h + 1]
        cum_row = running[h : h + 1, :]
        for low in (0, 256):
            high = low + 256
            scores = lax.dot_general(
                q_ref[low:high, head], k_ref[0:high, head], (((1,), (1,)), ((), ())),
                preferred_element_type=F32,
            )
            at_row = lax.broadcasted_iota(jnp.int32, (256, high), 0) + low
            at_col = lax.broadcasted_iota(jnp.int32, (256, high), 1)
            allowed = (at_row >= at_col) & (seg_col[low:high] == seg_row[:, 0:high])
            spread = cum_col[low:high] - cum_row[:, 0:high]
            weights = jnp.exp(jnp.where(allowed, spread, -1e30))
            mixing = (scores * weights).astype(BF16)
            within[h, low:high, :] = dot(mixing, v_ref[0:high, head])

    to_core.wait_recv()
    own = unpack(state_out, 0)
    own = (own_state, decay, seg_last)
    other = unpack(state_in, 0)
    first = choose(core == 0, own, other)
    second = choose(core == 0, other, own)
    chip = join(first, second)
    pack(1, *chip)
    to_y = []
    for index, by in enumerate((-1, 1, 2)):
        to_y.append(
            send(
                state_out.at[1], state_in.at[1 + index], state_send.at[1 + index],
                state_recv.at[1 + index], y_peer[by],
            )
        )
    load_res = load(7, res_hbm, res_ref)
    load_gain = load(8, gain_hbm, gain_ref)
    own_wh = load(9, wh_ref, wh.at[:, pl.ds(0, NV)])
    load_q.wait()
    inside(0)
    inside(1)
    fetch_1(0)
    fetch_1(1)
    for copy in to_y:
        copy.wait_recv()
    chips = {0: chip}
    for index, by in enumerate((1, -1, 2)):
        chips[by] = unpack(state_in, 1 + index)

    def chip_at(target):
        picked = chips[0]
        for by in (1, -1, 2):
            picked = choose(lax.rem(y + by + 4, 4) == target, chips[by], picked)
        return picked

    nothing = ([jnp.zeros((HD, HD), F32)] * 2, [jnp.ones((1, 1), F32)] * 2, jnp.zeros((1, 1), F32))
    total = chip_at(0)
    before = choose(y == 0, nothing, total)
    for target in range(1, 4):
        total = join(total, chip_at(target))
        before = choose(y > target, total, before)
    pack(2, *total)
    to_lo = send(state_out.at[2], state_in.at[4], state_send.at[4], state_recv.at[4], lo_peer)
    fetch_2(0)
    to_lo.wait_recv()
    earlier = unpack(state_in, 4)
    joined = choose(y == 0, earlier, join(earlier, before))
    before = choose(x_lo == 0, before, joined)
    fresh = (x_lo == 0) & (y == 0)
    with_first = choose(fresh, first, join(before, first))
    before = choose(core == 0, before, with_first)
    prior = before[2]

    sent_attn = []
    for h in range(2):
        head = slice(h * HD, (h + 1) * HD)
        scale = jnp.where(seg_col == prior, jnp.exp(columns[:, h : h + 1]), 0.0)
        carried = dot(q_ref[:, head], before[0][h].astype(BF16))
        output = within[h] + scale * carried
        mean = jnp.mean(output * output, axis=-1, keepdims=True)
        scaled = (output * lax.rsqrt(mean + EPSILON)).astype(BF16)
        for j in range(NZ):
            for half in range(2):
                low = (2 * j + half) * CH
                attn[h, half, j] = scaled[low : low + CH]
        sent_attn.append(
            send(attn.at[h, 1 - x_hi], attn_in.at[h], attn_send.at[h], attn_recv.at[h], hi_peer)
        )
    fetch_2(1)
    fetch_1(2)
    fetch_3(0)
    fetch_1(3)
    for d in range(NZ):
        chunk = lax.rem(z + d, NZ)
        rows = slice(d * CH, (d + 1) * CH)
        for h in range(2):
            lhs[rows, h * HD : (h + 1) * HD] = attn[h, x_hi, chunk]
    for slot, offset in enumerate(SLOT_OFFSET):
        chunk = lax.rem(z + offset + NZ, NZ)
        rows = pl.ds(pl.multiple_of((2 * chunk + x_hi) * CH, CH), CH)
        goals[slot * CH : (slot + 1) * CH, :] = columns[rows, :]
    for copy in sent_attn:
        copy.wait_recv()
    for piece in range(WO_PIECES, WO_PIECES + WH_PIECES):
        fetch_0(piece)
    for d in range(NZ):
        chunk = lax.rem(z + d, NZ)
        rows = slice(d * CH, (d + 1) * CH)
        for h in range(2):
            lhs[rows, 256 + h * HD : 256 + (h + 1) * HD] = attn_in[h, chunk]
    own_wo.wait()
    fetch_3(1)
    fetch_4(0)

    def project(sub):
        def tile(t, carry):
            cols = pl.ds(pl.multiple_of(sub * SUB + t * 512, 512), 512)
            part[:, :, cols] = dot(lhs[...], wo[:, cols]).reshape(NZ, CH, 512)
            return carry

        lax.fori_loop(0, SUB // 512, tile, 0)

    def as_row(column):
        wide = jnp.broadcast_to(column, (CH, HD))
        return jnp.concatenate([wide, jnp.zeros((HD - CH, HD), F32)], axis=0).T

    sums = {}

    def sum_send_to(way, step, sub):
        cols = slice(sub * SUB, (sub + 1) * SUB)
        value = part[SUM_SLOTS[way][step], :, cols]
        if (way, step - 1, sub) in sums:
            sums[way, step - 1, sub].wait_recv()
            value = value + landed[way, step - 1, :, cols].astype(F32)
        stage[way, step, :, cols] = value.astype(BF16)
        index = (way * 4 + step) * 4 + sub
        sums[way, step, sub] = send(
            stage.at[way, step, :, pl.ds(sub * SUB, SUB)],
            landed.at[way, step, :, pl.ds(sub * SUB, SUB)],
            sum_send.at[index], sum_recv.at[index], z_peer[1 if way == 0 else -1],
        )

    project(0)
    sum_send_to(0, 0, 0)
    sum_send_to(1, 1, 0)
    fetch_2(2)
    fetch_4(1)
    project(2)
    sum_send_to(1, 0, 2)
    sum_send_to(0, 1, 2)
    fetch_2(3)
    fetch_4(2)
    project(1)
    sum_send_to(0, 0, 1)
    sum_send_to(1, 1, 1)
    fetch_3(3)
    fetch_4(3)
    project(3)
    sum_send_to(1, 0, 3)
    sum_send_to(0, 1, 3)
    fetch_1(4)
    service = {
        3: [(fetch_1, 5)],
        6: [(fetch_2, 4), (fetch_1, 6)],
        8: [(fetch_2, 5), (fetch_1, 7)],
        9: [(fetch_1, 8)],
        10: [(fetch_3, 4), (fetch_2, 6)],
    }
    count = 2
    for step in range(1, 4):
        for i in (2, 3, 0, 1) if step > 1 else (0, 1):
            for way in range(2):
                sum_send_to(way, step, SUB_ORDER[way][i])
            for fetch, piece in service.get(count, ()):
                fetch(piece)
            count += 1

    gathers = {}

    def gather_to(way, step, sub):
        if step > 0:
            gathers[way, step - 1, sub].wait_recv()
        src = GATHER_FROM[way][step] * CH
        dst = GATHER_TO[way][step] * CH
        cols = pl.ds(sub * SUB, SUB)
        index = (way * 4 + step) * 4 + sub
        gathers[way, step, sub] = send(
            gathered.at[pl.ds(src, CH), cols], gathered.at[pl.ds(dst, CH), cols],
            gather_send.at[index], gather_recv.at[index], z_peer[1 if way == 0 else -1],
        )

    square = jnp.zeros((CH, 1), F32)
    load_res.wait()
    load_gain.wait()
    for sub in (2, 0, 3, 1):
        cols = slice(sub * SUB, (sub + 1) * SUB)
        for way in range(2):
            sums[way, 3, sub].wait_recv()
        value = part[0, :, cols] + landed[0, 3, :, cols].astype(F32)
        value = value + landed[1, 3, :, cols].astype(F32) + res_ref[:, cols].astype(F32)
        gathered[0:CH, cols] = (value * gain_ref[:, cols]).astype(BF16)
        for way in range(2):
            gather_to(way, 0, sub)
        square = square + jnp.sum(value * value, axis=1, keepdims=True)
    scale = lax.rsqrt(square / D + EPSILON)
    scales[0] = as_row(scale)[0:8, :]
    scale_moves = {}
    for slot in range(1, NZ):
        scale_moves[slot] = send(
            scales.at[0], scales.at[slot], scale_send.at[slot], scale_recv.at[slot],
            z_peer[SLOT_OFFSET[slot] if slot == NZ - 1 else -SLOT_OFFSET[slot]],
        )

    own_wh.wait()
    own_offset = vocab * NV
    other_offset = (z * 2 + 1 - x_hi) * NV

    def multiply(first, count, tile, subs=None, more=False):
        rows = slice(first * CH, (first + count) * CH)
        cols = slice(tile * TILE, (tile + 1) * TILE)
        if subs is None:
            logits[rows, cols] = dot(gathered[rows, :], wh[:, cols])
            return
        value = logits[rows, cols] if more else 0.0
        for sub in subs:
            deep = slice(sub * SUB, (sub + 1) * SUB)
            value = value + dot(gathered[rows, deep], wh[deep, cols])
        logits[rows, cols] = value

    def summarize(first, count):
        size = count * CH
        rows = slice(first * CH, (first + count) * CH)
        lines = []
        for slot in range(first, first + count):
            if slot > 0:
                scale_moves[slot].wait_recv()
            lines.append(scales[slot, 0:1, :])
        table = jnp.concatenate(lines + [jnp.zeros((HD - count, HD), F32)], axis=0).T
        factor = jnp.concatenate([table[0:CH, i : i + 1] for i in range(count)], axis=0)
        values = logits[rows, :] * factor
        top = jnp.max(values, axis=1, keepdims=True)
        mass = jnp.sum(jnp.exp(values - top), axis=1, keepdims=True)
        column = lax.broadcasted_iota(jnp.int32, (size, 2 * NV), 1)
        column = jnp.where(column < NV, column + own_offset, column - NV + other_offset)
        goal = goals[rows, 3:4].astype(jnp.int32)
        hit = jnp.sum(jnp.where(column == goal, values, 0.0), axis=1, keepdims=True)
        place = lax.broadcasted_iota(jnp.int32, (size, HD), 1)
        block = jnp.where(place == 0, top, jnp.where(place == 1, mass, hit))
        stats[rows, :] = block
        for slot in range(first, first + count):
            if slot > 0:
                stats_moves[slot] = send(
                    stats.at[pl.ds(slot * CH, CH)], stats_in.at[slot],
                    stats_send.at[slot], stats_recv.at[slot], z_peer[SLOT_OFFSET[slot]],
                )

    stats_moves = {}
    fetch_2(7)
    fetch_1(9)
    fetch_3(5)
    fetch_3(6)
    fetch_2(8)
    for i in range(4):
        for way in range(2):
            gather_to(way, 1, SUB_ORDER[way][i])
        if i == 0:
            fetch_3(7)
        if i == 1:
            fetch_3(8)
        if i == 2:
            fetch_2(9)
    for piece in range(WO_PIECES, WO_PIECES + WH_PIECES):
        fetch_4(piece)
    for i in range(4):
        multiply(0, 3, i)
        for way in range(2):
            gather_to(way, 2, SUB_ORDER[way][i])
    multiply(0, 3, 4)
    summarize(0, 3)
    for i in range(2):
        multiply(3, 2, i)
        for way in range(2):
            gather_to(way, 3, SUB_ORDER[way][i])
    for i in range(2, 5):
        multiply(3, 2, i)
    summarize(3, 2)
    for way in range(2):
        for i in range(2, 4):
            gathers[way, 2, SUB_ORDER[way][i]].wait_recv()
    for part_of in range(2):
        for way in range(2):
            gathers[way, 3, SUB_ORDER[way][part_of]].wait_recv()
        for i in range(5):
            multiply(5, 3, i, (part_of, part_of + 2), part_of > 0)
    summarize(5, 3)

    blocks = [stats[0:CH, :]]
    for slot in range(1, NZ):
        stats_moves[slot].wait_recv()
        blocks.append(stats_in[slot])
    top = blocks[0][:, 0:1]
    for block in blocks[1:]:
        top = jnp.maximum(top, block[:, 0:1])
    mass = jnp.zeros((CH, 1), F32)
    hit = jnp.zeros((CH, 1), F32)
    for block in blocks:
        mass = mass + block[:, 1:2] * jnp.exp(block[:, 0:1] - top)
        hit = hit + block[:, 2:3]
    out_ref[...] = as_row(hit - top - jnp.log(mass))[0:1, 0:CH]
    for copy in waiting:
        copy.wait_send()


def shards(
    query_rows, key_rows, value_rows, log_decay, segment_ids, residual, out_weight, final_gain,
    head_weight, targets,
):
    vmem = pl.BlockSpec(memory_space=pltpu.VMEM)
    hbm = pl.BlockSpec(memory_space=pl.ANY)
    dma = pltpu.SemaphoreType.DMA
    pieces = WO_PIECES + WH_PIECES
    result = pl.pallas_call(
        kernel,
        out_shape=jax.ShapeDtypeStruct((1, CH), F32),
        in_specs=[hbm] * 10,
        out_specs=vmem,
        scratch_shapes=[
            pltpu.VMEM((TOK, 2 * HD), BF16),
            pltpu.VMEM((TOK, 2 * HD), BF16),
            pltpu.VMEM((TOK, 2 * HD), BF16),
            pltpu.VMEM((2, TOK), F32),
            pltpu.VMEM((1, TOK), jnp.int32),
            pltpu.VMEM((1, TOK), jnp.int32),
            pltpu.VMEM((CH, D), BF16),
            pltpu.VMEM((1, D), F32),
            pltpu.VMEM((512, D), BF16),
            pltpu.VMEM((D, 2 * NV), BF16),
            pltpu.VMEM((NZ, CH, D), F32),
            pltpu.VMEM((2, 4, CH, D), BF16),
            pltpu.VMEM((2, 4, CH, D), BF16),
            pltpu.VMEM((NZ * CH, D), BF16),
            pltpu.VMEM((NZ * CH, 2 * NV), F32),
            pltpu.VMEM((NZ, 8, HD), F32),
            pltpu.VMEM((2, TOK, HD), F32),
            pltpu.VMEM((TOK, HD), F32),
            pltpu.VMEM((NZ * CH, HD), F32),
            pltpu.VMEM((2, 2, NZ, CH, HD), BF16),
            pltpu.VMEM((2, NZ, CH, HD), BF16),
            pltpu.VMEM((NZ * CH, 512), BF16),
            pltpu.VMEM((3, 2 * HD + 16, HD), BF16),
            pltpu.VMEM((5, 2 * HD + 16, HD), BF16),
            pltpu.VMEM((NZ * CH, HD), F32),
            pltpu.VMEM((NZ, CH, HD), F32),
            dma((10,)),
            dma((pieces, 9)),
            dma((pieces, 9)),
            dma((5,)),
            dma((5,)),
            dma((2,)),
            dma((2,)),
            dma((32,)),
            dma((32,)),
            dma((32,)),
            dma((32,)),
            dma((NZ,)),
            dma((NZ,)),
            dma((NZ,)),
            dma((NZ,)),
        ],
        compiler_params=pltpu.CompilerParams(
            collective_id=0, has_side_effects=True, vmem_limit_bytes=56 * 1024 * 1024
        ),
        name="layer",
    )(
        query_rows, key_rows, value_rows, log_decay, segment_ids.reshape(1, -1),
        targets.reshape(1, -1), residual, final_gain.reshape(1, -1), out_weight, head_weight,
    )
    return result.reshape(CH)


def solution(mesh):
    in_specs = (
        P("ctx", "vocab"),
        P("ctx", "vocab"),
        P("ctx", "vocab"),
        P("vocab", "ctx"),
        P("ctx"),
        P(("ctx", "vocab"), None),
        P("vocab", None),
        P(),
        P(None, "vocab"),
        P("ctx"),
    )
    out_specs = P(("ctx", "vocab"))
    return jax.shard_map(shards, mesh=mesh, in_specs=in_specs, out_specs=out_specs, check_vma=False)
```

```python
import jax
import jax.numpy as jnp
from jax import lax
from jax.experimental import pallas as pl
from jax.experimental.pallas import tpu as pltpu
from jax.sharding import PartitionSpec as P

EPSILON = 1e-06
MESH = pl.DeviceIdType.MESH
F32 = jnp.float32
BF16 = jnp.bfloat16

TOK = 512
D = 6144
HD = 128
NV = 640
CH = 32
NZ = 8
HALF = 256
DZ = 768
TILE = 256
COPIES = 192

SLOT_OFFSET = (0, -1, 1, -2, 2, -3, 3, 4)
GATHER_FROM = ((0, 1, 3, 5), (0, 2, 4, 6))
GATHER_TO = ((1, 3, 5, 7), (2, 4, 6, 7))

KINDS = "XYYYYY"
WH_ROWS = 1024


def dot(a, b):
    return jnp.dot(a, b, preferred_element_type=F32)


def kernel(
    q_hbm, k_hbm, v_hbm, ld_hbm, seg_hbm, tgt_hbm, res_hbm, gain_hbm, wo_ref, wh_ref,
    out_ref,
    q_ref, k_ref, v_ref, ld_ref, seg_ref, tgt_ref, res, gain_ref,
    wo, wh, attn, heads, partial, swap_out, swap_in, slices, logits, squares, within, columns, goals,
    state_out, state_in, stats, stats_out, stats_in,
    local_sem, send_sem, recv_sem,
):
    ctx = lax.axis_index("ctx")
    vocab = lax.axis_index("vocab")
    x_lo = ctx // 8
    y = lax.rem(ctx // 2, 4)
    core = lax.rem(ctx, 2)
    z = vocab // 2
    x_hi = lax.rem(vocab, 2)

    def at_y(by):
        return x_lo * 8 + lax.rem(y + by + 4, 4) * 2 + core

    def along_z(by):
        return lax.rem(z + by + NZ, NZ)

    sibling = (ctx + 1 - 2 * core, vocab)
    y_peer = {by: (at_y(by), vocab) for by in (-1, 1, 2)}
    lo_peer = (lax.rem(ctx + 8, 16), vocab)
    cut_peer = (lax.rem(ctx + 8, 16), z * 2 + 1 - x_hi)
    hi_peer = (ctx, z * 2 + 1 - x_hi)
    z_peer = {by: (ctx, along_z(by) * 2 + x_hi) for by in (-3, -2, -1, 1, 2, 3, 4)}

    barrier = pltpu.get_barrier_semaphore()
    peers = [sibling, lo_peer, cut_peer, hi_peer, *y_peer.values(), *z_peer.values()]
    for peer in peers:
        pl.semaphore_signal(barrier, inc=1, device_id=peer, device_id_type=MESH)

    def load(index, src, dst):
        copy = pltpu.make_async_copy(src, dst, local_sem.at[index])
        copy.start()
        return copy

    small = [
        load(0, ld_hbm, ld_ref), load(1, seg_hbm, seg_ref), load(2, tgt_hbm, tgt_ref),
        load(3, k_hbm, k_ref), load(4, v_hbm, v_ref),
    ]
    load_q = load(5, q_hbm, q_ref)

    moves = {}

    def move(name, src, dst, peer):
        index = len(moves)
        copy = pltpu.make_async_remote_copy(
            src_ref=src, dst_ref=dst, send_sem=send_sem.at[index], recv_sem=recv_sem.at[index],
            device_id=peer, device_id_type=MESH,
        )
        copy.start()
        moves[name] = copy

    def arrived(*name):
        moves[name].wait_recv()

    def strip(at_lo, at_row, of_core):
        return of_core * 8 + at_lo * 4 + at_row

    def item(lo, by, first=0, count=NZ):
        row = lax.rem(y + by + 4, 4)
        return wo.at[pl.ds(first, count), strip(lax.rem(x_lo + lo, 2), row, core)]

    own_strip = strip(x_lo, y, core)

    def pass_item(name, lo, by, peer, first=0, count=NZ):
        view = item(lo, by, first, count)
        move(name, view, view, peer)

    def wo_0():
        rows = pl.ds(pl.multiple_of(own_strip * 16, 16), 16)
        for by in (1, -1, 2, -2, 3, -3, 4):
            cols = pl.ds(pl.multiple_of(along_z(by) * DZ, 128), DZ)
            move(("wz", by), wo_ref.at[rows, cols], wo.at[z, own_strip], z_peer[by])
        cols = pl.ds(pl.multiple_of(z * DZ, 128), DZ)
        return load(6, wo_ref.at[rows, cols], wo.at[z, own_strip])

    def to_core(lo, by):
        pass_item(("core", lo, by), lo, by, sibling)

    def wo_1():
        for by in (1, -1, 2, -2, 3, -3, 4):
            arrived("wz", by)
        own_strip_copy.wait()
        pass_item(("up", 0), 0, 0, y_peer[1])
        pass_item(("down", 0), 0, 0, y_peer[-1])
        pass_item(("lo", 0), 0, 0, lo_peer)
        to_core(0, 0)

    def wo_2():
        arrived("up", 0)
        pass_item(("up2", 0), 0, -1, y_peer[1], 0, 4)
        pass_item(("lo", -1), 0, -1, lo_peer, 0, 4)
        to_core(0, -1)
        arrived("down", 0)
        pass_item(("down2", 0), 0, 1, y_peer[-1], 4, 4)
        pass_item(("lo", 1), 0, 1, lo_peer, 0, 4)
        to_core(0, 1)

    def wo_3():
        arrived("lo", 0)
        pass_item(("up", 1), 1, 0, y_peer[1], 4, 4)
        pass_item(("down", 1), 1, 0, y_peer[-1], 4, 4)
        to_core(1, 0)

    def wo_4():
        arrived("up2", 0)
        arrived("down2", 0)
        pass_item(("lo", 2), 0, 2, lo_peer, 0, 4)
        to_core(0, 2)
        arrived("up", 1)
        pass_item(("up2", 1), 1, -1, y_peer[1], 4, 2)
        arrived("lo", -1)
        to_core(1, -1)
        arrived("down", 1)
        pass_item(("down2", 1), 1, 1, y_peer[-1], 6, 2)
        arrived("lo", 1)
        to_core(1, 1)

    def wo_5():
        arrived("up2", 1)
        arrived("down2", 1)
        arrived("lo", 2)
        to_core(1, 2)

    def wo_6():
        for lo in range(2):
            for by in (0, -1, 1, 2):
                arrived("core", lo, by)

    def part_rows(piece):
        return WH_ROWS // (8 if KINDS[piece] == "Y" else 4)

    def part_start(piece, by):
        if KINDS[piece] == "Y":
            index = lax.rem(y + by + 4, 4) * 2 + core
        else:
            index = lax.rem(x_lo + by, 2) * 2 + core
        return index * part_rows(piece) + piece * WH_ROWS

    def piece_view(piece, by, low=0, size=None):
        size = part_rows(piece) if size is None else size
        return wh.at[pl.ds(pl.multiple_of(part_start(piece, by) + low, 16), size), pl.ds(NV, NV)]

    def fetch_0(piece):
        by = 0 if KINDS[piece] == "Y" else 1
        rows = pl.ds(pl.multiple_of(part_start(piece, by), 16), part_rows(piece))
        move(("cut", piece), wh_ref.at[rows, :], piece_view(piece, by), cut_peer)

    def fetch_1(piece):
        arrived("cut", piece)
        view = piece_view(piece, 0)
        if KINDS[piece] == "Y":
            move(("wup", piece), view, view, y_peer[1])
            move(("wdown", piece), view, view, y_peer[-1])
        else:
            move(("wlo", piece), view, view, lo_peer)
        move(("core0", piece), view, view, sibling)

    def fetch_2(piece):
        if KINDS[piece] == "X":
            arrived("wlo", piece)
            view = piece_view(piece, 1)
            move(("core1", piece), view, view, sibling)
            return
        half = part_rows(piece) // 2
        arrived("wup", piece)
        view = piece_view(piece, -1, 0, half)
        move(("wup2", piece), view, view, y_peer[1])
        view = piece_view(piece, -1)
        move(("core1", piece), view, view, sibling)
        arrived("wdown", piece)
        view = piece_view(piece, 1, half, half)
        move(("wdown2", piece), view, view, y_peer[-1])
        view = piece_view(piece, 1)
        move(("core2", piece), view, view, sibling)

    def fetch_3(piece):
        arrived("wup2", piece)
        arrived("wdown2", piece)
        view = piece_view(piece, 2)
        move(("core3", piece), view, view, sibling)

    def fetch_4(piece):
        for name in ("core0", "core1", "core2", "core3"):
            if (name, piece) in moves:
                arrived(name, piece)

    for copy in small:
        copy.wait()

    lane = lax.broadcasted_iota(jnp.int32, (8, TOK), 1)
    running = jnp.concatenate([ld_ref[...], jnp.zeros((6, TOK), F32)], axis=0)
    shift = 1
    while shift < TOK:
        running = running + jnp.where(lane >= shift, pltpu.roll(running, shift, axis=1), 0.0)
        shift *= 2
    seg_row = seg_ref[...].astype(F32)
    table = jnp.concatenate(
        [running[0:2], seg_row, tgt_ref[...].astype(F32), jnp.zeros((124, TOK), F32)], axis=0
    )
    columns[...] = table.T
    seg_col = columns[:, 2:3]
    seg_last = seg_col[TOK - 1 : TOK, :]

    decay = []
    own_state = []
    for h in range(2):
        head = slice(h * HD, (h + 1) * HD)
        cum_col = columns[:, h : h + 1]
        last = cum_col[TOK - 1 : TOK, :]
        tail = jnp.where(seg_col == seg_last, jnp.exp(last - cum_col), 0.0)
        weighted = (k_ref[:, head].astype(F32) * tail).astype(BF16)
        summary = lax.dot_general(
            weighted, v_ref[:, head], (((0,), (0,)), ((), ())), preferred_element_type=F32
        )
        own_state.append(summary)
        decay.append(jnp.exp(last))

    def pack(slot, states, decays, seg):
        for h in range(2):
            state_out[slot, h * HD : (h + 1) * HD, :] = states[h].astype(BF16)
        row = lax.broadcasted_iota(jnp.int32, (16, HD), 0)
        tops = [d.astype(BF16).astype(F32) for d in decays]
        block = jnp.where(row == 0, tops[0], 0.0)
        block = jnp.where(row == 1, decays[0] - tops[0], block)
        block = jnp.where(row == 2, tops[1], block)
        block = jnp.where(row == 3, decays[1] - tops[1], block)
        block = jnp.where(row == 4, seg, block)
        state_out[slot, 2 * HD : 2 * HD + 16, :] = block.astype(BF16)

    def unpack(buffer, slot):
        states = [buffer[slot, h * HD : (h + 1) * HD, :].astype(F32) for h in range(2)]
        block = buffer[slot, 2 * HD : 2 * HD + 16, :].astype(F32)
        decays = [block[0:1, 0:1] + block[1:2, 0:1], block[2:3, 0:1] + block[3:4, 0:1]]
        return states, decays, block[4:5, 0:1]

    def join(first, second):
        states = [
            jnp.where(first[2] == second[2], second[1][h], 0.0) * first[0][h] + second[0][h]
            for h in range(2)
        ]
        return states, [first[1][h] * second[1][h] for h in range(2)], second[2]

    def choose(flag, a, b):
        return (
            [jnp.where(flag, a[0][h], b[0][h]) for h in range(2)],
            [jnp.where(flag, a[1][h], b[1][h]) for h in range(2)],
            jnp.where(flag, a[2], b[2]),
        )

    pack(0, own_state, decay, seg_last)
    pl.semaphore_wait(barrier, len(peers))
    move(("core",), state_out.at[0], state_in.at[0], sibling)
    own_strip_copy = wo_0()
    for by in (1, -1, 2, -2, 3, -3, 4):
        cols = pl.ds(pl.multiple_of(along_z(by) * DZ, 128), DZ)
        move(("res", by), res_hbm.at[:, cols], res.at[z], z_peer[by])
    cols = pl.ds(pl.multiple_of(z * DZ, 128), DZ)
    own_res = load(7, res_hbm.at[:, cols], res.at[z])
    load_gain = load(8, gain_hbm.at[:, cols], gain_ref)
    for piece in range(len(KINDS)):
        fetch_0(piece)
    own_wh = load(9, wh_ref, wh.at[:, pl.ds(0, NV)])

    def inside(h):
        head = slice(h * HD, (h + 1) * HD)
        cum_col = columns[:, h : h + 1]
        cum_row = running[h : h + 1, :]
        for low in (0, 256):
            high = low + 256
            scores = lax.dot_general(
                q_ref[low:high, head], k_ref[0:high, head], (((1,), (1,)), ((), ())),
                preferred_element_type=F32,
            )
            at_row = lax.broadcasted_iota(jnp.int32, (256, high), 0) + low
            at_col = lax.broadcasted_iota(jnp.int32, (256, high), 1)
            allowed = (at_row >= at_col) & (seg_col[low:high] == seg_row[:, 0:high])
            spread = cum_col[low:high] - cum_row[:, 0:high]
            weights = jnp.exp(jnp.where(allowed, spread, -1e30))
            mixing = (scores * weights).astype(BF16)
            within[h, low:high, :] = dot(mixing, v_ref[0:high, head])

    arrived("core")

    own = (own_state, decay, seg_last)
    other = unpack(state_in, 0)
    first = choose(core == 0, own, other)
    second = choose(core == 0, other, own)
    chip = join(first, second)
    pack(1, *chip)
    for index, by in enumerate((-1, 1, 2)):
        move(("state", by), state_out.at[1], state_in.at[1 + index], y_peer[by])
    load_q.wait()
    inside(0)
    inside(1)
    for by in (-1, 1, 2):
        arrived("state", by)
    chips = {0: chip}
    for index, by in enumerate((1, -1, 2)):
        chips[by] = unpack(state_in, 1 + index)

    def chip_at(target):
        picked = chips[0]
        for by in (1, -1, 2):
            picked = choose(lax.rem(y + by + 4, 4) == target, chips[by], picked)
        return picked

    nothing = ([jnp.zeros((HD, HD), F32)] * 2, [jnp.ones((1, 1), F32)] * 2, jnp.zeros((1, 1), F32))
    total = chip_at(0)
    before = choose(y == 0, nothing, total)
    for target in range(1, 4):
        total = join(total, chip_at(target))
        before = choose(y > target, total, before)
    pack(2, *total)
    move(("total",), state_out.at[2], state_in.at[4], lo_peer)
    wo_1()
    arrived("total")
    earlier = unpack(state_in, 4)
    joined = choose(y == 0, earlier, join(earlier, before))
    before = choose(x_lo == 0, before, joined)
    fresh = (x_lo == 0) & (y == 0)
    with_first = choose(fresh, first, join(before, first))
    before = choose(core == 0, before, with_first)
    prior = before[2]


    def own_heads(sub):
        return attn.at[sub % 2, 1 - x_hi if sub < 2 else x_hi]

    def gather_heads(way, step, sub):
        if step > 0:
            arrived("heads", way, step - 1, sub)
        src = own_heads(sub) if step == 0 else heads.at[GATHER_FROM[way][step], sub]
        dst = heads.at[GATHER_TO[way][step], sub]
        move(("heads", way, step, sub), src, dst, z_peer[1 if way == 0 else -1])

    for h in range(2):
        head = slice(h * HD, (h + 1) * HD)
        scale = jnp.where(seg_col == prior, jnp.exp(columns[:, h : h + 1]), 0.0)
        carried = dot(q_ref[:, head], before[0][h].astype(BF16))
        output = within[h] + scale * carried
        mean = jnp.mean(output * output, axis=-1, keepdims=True)
        scaled = (output * lax.rsqrt(mean + EPSILON)).astype(BF16)
        for j in range(NZ):
            for half in range(2):
                low = (2 * j + half) * CH
                attn[h, half, j * CH : (j + 1) * CH] = scaled[low : low + CH]
    for sub in range(4):
        for way in range(2):
            gather_heads(way, 0, sub)
    wo_2()
    wo_3()
    for j in range(NZ):
        rows = pl.ds(pl.multiple_of((2 * j + x_hi) * CH, CH), CH)
        goals[j * CH : (j + 1) * CH, :] = columns[rows, :]
    for sub in range(2):
        for way in range(2):
            gather_heads(way, 1, sub)
    wo_4()
    for sub in range(2, 4):
        for way in range(2):
            gather_heads(way, 1, sub)
    wo_5()
    fetch_1(0)
    for sub in range(4):
        for way in range(2):
            gather_heads(way, 2, sub)
        if sub == 0:
            fetch_1(1)
            fetch_1(2)
        if sub == 2:
            fetch_1(3)
            fetch_1(4)
    wo_6()

    def project(slot, near):
        if slot == 0:
            left = jnp.concatenate([own_heads(2 * near + h)[...] for h in range(2)], axis=1)
        else:
            left = jnp.concatenate([heads[slot, 2 * near + h] for h in range(2)], axis=1)
        return dot(left, wo[along_z(SLOT_OFFSET[slot])].reshape(HALF, DZ))

    for near in range(2):
        partial[near] = project(0, near) + project(1, near) + project(2, near)
    for sub in (0, 2):
        gather_heads(0, 3, sub)
        gather_heads(1, 3, sub + 1)
    fetch_1(5)
    for near in range(2):
        partial[near] += project(3, near) + project(4, near)
    own_res.wait()
    load_gain.wait()
    for by in (1, -1, 2, -2, 3, -3, 4):
        arrived("res", by)
    partial[1] += res[...].reshape(HALF, DZ).astype(F32)
    for sub in (0, 2):
        arrived("heads", 1, 2, sub)
        arrived("heads", 0, 2, sub + 1)
    for near in range(2):
        partial[near] += project(5, near) + project(6, near)
    arrived("heads", 0, 3, 0)
    arrived("heads", 1, 3, 1)
    far = partial[0] + project(7, 0)
    for sub in range(4):
        rows = slice(sub * 64, (sub + 1) * 64)
        swap_out[rows, :] = far[rows].astype(BF16)
        view = pl.ds(sub * 64, 64)
        move(("swap", sub), swap_out.at[view], swap_in.at[view], hi_peer)
    arrived("heads", 0, 3, 2)
    arrived("heads", 1, 3, 3)
    partial[1] += project(7, 1)

    def sub_rows(sub):
        return pl.ds(sub * 64, 64)

    def gather_hidden(way, step, sub):
        if step > 0:
            arrived("hidden", way, step - 1, sub)
        src = slices.at[GATHER_FROM[way][step], sub_rows(sub)]
        dst = slices.at[GATHER_TO[way][step], sub_rows(sub)]
        move(("hidden", way, step, sub), src, dst, z_peer[1 if way == 0 else -1])

    order = ((0, 2, 1, 3), (1, 3, 0, 2))
    for sub in range(4):
        arrived("swap", sub)
        rows = slice(sub * 64, (sub + 1) * 64)
        value = partial[1, rows, :] + swap_in[rows, :].astype(F32)
        partial[1, rows, :] = value
        slices[0, rows, :] = (value * gain_ref[...]).astype(BF16)
        for way in range(2):
            gather_hidden(way, 0, sub)
    square = jnp.sum(partial[1] * partial[1], axis=1, keepdims=True)
    turned = jnp.broadcast_to(square, (HALF, HD)).T
    squares[0] = jnp.concatenate(
        [turned[0:1, 0:HD], turned[0:1, HD:HALF], jnp.zeros((6, HD), F32)], axis=0
    )
    for slot in range(1, NZ):
        offset = SLOT_OFFSET[slot]
        peer = z_peer[offset if slot == NZ - 1 else -offset]
        move(("square", slot), squares.at[0], squares.at[slot], peer)

    own_offset = vocab * NV
    other_offset = (z * 2 + 1 - x_hi) * NV

    def multiply(slots, low, high, cols, more=True):
        value = logits[low:high, cols] if more else 0.0
        for slot in slots:
            deep = pl.ds(pl.multiple_of(along_z(SLOT_OFFSET[slot]) * DZ, DZ), DZ)
            value = value + dot(slices[slot, low:high, :], wh[deep, cols])
        logits[low:high, cols] = value

    def summarize(low, high):
        size = high - low
        values = logits[low:high, :] * factor[low:high]
        top = jnp.max(values, axis=1, keepdims=True)
        mass = jnp.sum(jnp.exp(values - top), axis=1, keepdims=True)
        column = lax.broadcasted_iota(jnp.int32, (size, 2 * NV), 1)
        column = jnp.where(column < NV, column + own_offset, column - NV + other_offset)
        goal = goals[low:high, 3:4].astype(jnp.int32)
        hit = jnp.sum(jnp.where(column == goal, values, 0.0), axis=1, keepdims=True)
        lane_of = lax.broadcasted_iota(jnp.int32, (size, HD), 1)
        stats[low:high, :] = jnp.where(lane_of == 0, top, jnp.where(lane_of == 1, mass, hit))

    own_tiles = (slice(0, 256), slice(256, 512), slice(512, 640))
    other_tiles = (slice(640, 896), slice(896, 1152), slice(1152, 1280))
    all_tiles = tuple(slice(i * TILE, (i + 1) * TILE) for i in range(5))
    own_wh.wait()
    fetch_2(0)
    service = {
        (1, 0): [(fetch_2, 1), (fetch_2, 2)],
        (1, 1): [(fetch_2, 3)],
        (1, 2): [(fetch_2, 4)],
        (1, 3): [(fetch_2, 5)],
        (2, 0): [(fetch_3, 1)],
        (2, 1): [(fetch_3, 2)],
        (2, 2): [(fetch_3, 3), (fetch_3, 4)],
        (2, 3): [(fetch_3, 5)],
    }
    for step in (1, 2):
        for i in range(4):
            for way in range(2):
                gather_hidden(way, step, order[way][i])
            for fetch, piece in service.get((step, i), ()):
                fetch(piece)
    for i in range(2):
        for way in range(2):
            gather_hidden(way, 3, order[way][i])
    for tile in own_tiles:
        multiply((0, 1, 2, 3, 4), 0, HALF, tile, False)
    for piece in range(len(KINDS)):
        fetch_4(piece)
    for tile in other_tiles:
        multiply((0, 1, 2, 3, 4), 0, HALF, tile, False)
    total_square = squares[0]
    for slot in range(1, NZ):
        arrived("square", slot)
        total_square = total_square + squares[slot]
    factor = lax.rsqrt(total_square / D + EPSILON)
    factor = jnp.concatenate([factor, jnp.zeros((HD - 8, HD), F32)], axis=0).T
    factor = jnp.concatenate([factor[:, 0:1], factor[:, 1:2]], axis=0)
    for way in range(2):
        for i in range(2, 4):
            arrived("hidden", way, 2, order[way][i])
    for tile in all_tiles:
        multiply((5, 6), 0, HALF, tile)
    for i in range(2):
        for way in range(2):
            arrived("hidden", way, 3, order[way][i])
        for tile in all_tiles:
            multiply((7,), i * 128, i * 128 + 128, tile)
        summarize(i * 128, i * 128 + 128)
    turned = stats[...].T
    for half in range(2):
        stats_out[half] = turned[0:8, half * HD : (half + 1) * HD]
    for by in (4, 3, -3, 2, -2, 1, -1):
        move(("stats", by), stats_out.at[along_z(by) // 4], stats_in.at[by + 3], z_peer[by])
    blocks = [stats_out[z // 4]]
    for by in (1, -1, 2, -2, 3, -3, 4):
        arrived("stats", by)
        blocks.append(stats_in[by + 3])
    top = blocks[0][0:1]
    for block in blocks[1:]:
        top = jnp.maximum(top, block[0:1])
    mass = jnp.zeros((1, HD), F32)
    hit = jnp.zeros((1, HD), F32)
    for block in blocks:
        mass = mass + block[1:2] * jnp.exp(block[0:1] - top)
        hit = hit + block[2:3]
    result = hit - top - jnp.log(mass)
    quarter = lax.rem(z, 4)
    picked = result[:, 0:CH]
    for i in range(1, 4):
        picked = jnp.where(quarter == i, result[:, i * CH : (i + 1) * CH], picked)
    out_ref[...] = picked
    for copy in moves.values():
        copy.wait_send()


def shards(
    query_rows, key_rows, value_rows, log_decay, segment_ids, residual, out_weight, final_gain,
    head_weight, targets,
):
    vmem = pl.BlockSpec(memory_space=pltpu.VMEM)
    hbm = pl.BlockSpec(memory_space=pl.ANY)
    dma = pltpu.SemaphoreType.DMA
    result = pl.pallas_call(
        kernel,
        out_shape=jax.ShapeDtypeStruct((1, CH), F32),
        in_specs=[hbm] * 10,
        out_specs=vmem,
        scratch_shapes=[
            pltpu.VMEM((TOK, 2 * HD), BF16),
            pltpu.VMEM((TOK, 2 * HD), BF16),
            pltpu.VMEM((TOK, 2 * HD), BF16),
            pltpu.VMEM((2, TOK), F32),
            pltpu.VMEM((1, TOK), jnp.int32),
            pltpu.VMEM((1, TOK), jnp.int32),
            pltpu.VMEM((NZ, CH, DZ), BF16),
            pltpu.VMEM((1, DZ), F32),
            pltpu.VMEM((NZ, 16, 16, DZ), BF16),
            pltpu.VMEM((D, 2 * NV), BF16),
            pltpu.VMEM((2, 2, HALF, HD), BF16),
            pltpu.VMEM((NZ, 4, HALF, HD), BF16),
            pltpu.VMEM((2, HALF, DZ), F32),
            pltpu.VMEM((HALF, DZ), BF16),
            pltpu.VMEM((HALF, DZ), BF16),
            pltpu.VMEM((NZ, HALF, DZ), BF16),
            pltpu.VMEM((HALF, 2 * NV), F32),
            pltpu.VMEM((NZ, 8, HD), F32),
            pltpu.VMEM((2, TOK, HD), F32),
            pltpu.VMEM((TOK, HD), F32),
            pltpu.VMEM((HALF, HD), F32),
            pltpu.VMEM((3, 2 * HD + 16, HD), BF16),
            pltpu.VMEM((5, 2 * HD + 16, HD), BF16),
            pltpu.VMEM((HALF, HD), F32),
            pltpu.VMEM((2, 8, HD), F32),
            pltpu.VMEM((NZ, 8, HD), F32),
            dma((10,)),
            dma((COPIES,)),
            dma((COPIES,)),
        ],
        compiler_params=pltpu.CompilerParams(
            collective_id=0, has_side_effects=True, vmem_limit_bytes=56 * 1024 * 1024
        ),
        name="layer",
    )(
        query_rows, key_rows, value_rows, log_decay, segment_ids.reshape(1, -1),
        targets.reshape(1, -1), residual, final_gain.reshape(1, -1), out_weight, head_weight,
    )
    return result.reshape(CH)


def solution(mesh):
    in_specs = (
        P("ctx", "vocab"),
        P("ctx", "vocab"),
        P("ctx", "vocab"),
        P("vocab", "ctx"),
        P("ctx"),
        P(("ctx", "vocab"), None),
        P("vocab", None),
        P(),
        P(None, "vocab"),
        P("ctx"),
    )
    out_specs = P(("ctx", "vocab"))
    return jax.shard_map(shards, mesh=mesh, in_specs=in_specs, out_specs=out_specs, check_vma=False)
```

```python
import jax
import jax.numpy as jnp
from jax import lax
from jax.experimental import pallas as pl
from jax.experimental.pallas import tpu as pltpu
from jax.sharding import PartitionSpec as P

EPSILON = 1e-06
MESH = pl.DeviceIdType.MESH
F32 = jnp.float32
BF16 = jnp.bfloat16

TOK = 512
D = 6144
HD = 128
NV = 640
CH = 32
NZ = 8
HALF = 256
DZ = 768
TILE = 256
ARRIVALS = 65
GROUPS = ("state", "res", "strip", "wo", "wh", "heads", "swap", "hidden", "square", "stats")

OTHERS = (1, -1, 2, -2, 3, -3, 4)
SLOT_OFFSET = (0, -1, 1, -2, 2, -3, 3, 4)
GATHER_FROM = ((0, 1, 3, 5), (0, 2, 4, 6))
GATHER_TO = ((1, 3, 5, 7), (2, 4, 6, 7))

KINDS = "XYYYYY"
WH_ROWS = 1024


def dot(a, b):
    return jnp.dot(a, b, preferred_element_type=F32)


def kernel(
    q_hbm, k_hbm, v_hbm, ld_hbm, seg_hbm, tgt_hbm, res_hbm, gain_hbm, wo_ref, wh_ref,
    out_ref,
    q_ref, k_ref, v_ref, ld_ref, seg_ref, tgt_ref, res, gain_ref,
    wo, wh, attn, heads, partial, hidden, swap_out, swap_in, slices, logits, squares, within, columns, goals,
    state_out, state_in, stats, stats_out, stats_in,
    local_sem, send_sem, recv_sem,
):
    ctx = lax.axis_index("ctx")
    vocab = lax.axis_index("vocab")
    x_lo = ctx // 8
    y = lax.rem(ctx // 2, 4)
    core = lax.rem(ctx, 2)
    z = vocab // 2
    x_hi = lax.rem(vocab, 2)

    def at_y(by):
        return x_lo * 8 + lax.rem(y + by + 4, 4) * 2 + core

    def along_z(by):
        return lax.rem(z + by + NZ, NZ)

    sibling = (ctx + 1 - 2 * core, vocab)
    y_peer = {by: (at_y(by), vocab) for by in (-1, 1, 2)}
    lo_peer = (lax.rem(ctx + 8, 16), vocab)
    cut_peer = (lax.rem(ctx + 8, 16), z * 2 + 1 - x_hi)
    hi_peer = (ctx, z * 2 + 1 - x_hi)
    z_peer = {by: (ctx, along_z(by) * 2 + x_hi) for by in (-3, -2, -1, 1, 2, 3, 4)}

    barrier = pltpu.get_barrier_semaphore()
    peers = [sibling, lo_peer, cut_peer, hi_peer, *y_peer.values(), *z_peer.values()]
    for peer in peers:
        pl.semaphore_signal(barrier, inc=1, device_id=peer, device_id_type=MESH)

    def load(index, src, dst):
        copy = pltpu.make_async_copy(src, dst, local_sem.at[index])
        copy.start()
        return copy

    small = [
        load(0, ld_hbm, ld_ref), load(1, seg_hbm, seg_ref), load(2, tgt_hbm, tgt_ref),
        load(3, k_hbm, k_ref), load(4, v_hbm, v_ref),
    ]
    load_q = load(5, q_hbm, q_ref)

    arrivals = {}

    def move(group, key, src, dst, peer):
        index = arrivals.setdefault(key, len(arrivals))
        pltpu.make_async_remote_copy(
            src_ref=src, dst_ref=dst, send_sem=send_sem.at[GROUPS.index(group)],
            recv_sem=recv_sem.at[index], device_id=peer, device_id_type=MESH,
        ).start()

    def arrived(like, *key):
        pltpu.make_async_copy(like, like, recv_sem.at[arrivals[key]]).wait()

    def departed(like, group):
        pltpu.make_async_copy(like, like, send_sem.at[GROUPS.index(group)]).wait()

    def strip(at_lo, at_row, of_core):
        return of_core * 8 + at_lo * 4 + at_row

    def item(lo, by, first=0, count=NZ):
        row = lax.rem(y + by + 4, 4)
        return wo.at[pl.ds(first, count), strip(lax.rem(x_lo + lo, 2), row, core)]

    own_strip = strip(x_lo, y, core)

    def pass_item(key, lo, by, peer, first=0, count=NZ):
        view = item(lo, by, first, count)
        move("wo", key, view, view, peer)

    def wo_0():
        rows = pl.ds(pl.multiple_of(own_strip * 16, 16), 16)
        for by in OTHERS:
            cols = pl.ds(pl.multiple_of(along_z(by) * DZ, 128), DZ)
            move("strip", ("z",), wo_ref.at[rows, cols], wo.at[z, own_strip], z_peer[by])
        cols = pl.ds(pl.multiple_of(z * DZ, 128), DZ)
        return load(6, wo_ref.at[rows, cols], wo.at[z, own_strip])

    one_item = wo.at[0, pl.ds(0, 8)]

    def to_core(lo, by):
        view = item(lo, by)
        move("strip" if (lo, by) == (0, 0) else "wo", ("core",), view, view, sibling)

    def wo_1():
        arrived(wo.at[0, pl.ds(0, NZ - 1)], "z")
        own_strip_copy.wait()
        pass_item(("up",), 0, 0, y_peer[1])
        pass_item(("down",), 0, 0, y_peer[-1])
        pass_item(("lo",), 0, 0, lo_peer)
        to_core(0, 0)

    def wo_2():
        arrived(one_item, "up")
        pass_item(("far",), 0, -1, y_peer[1], 0, 4)
        pass_item(("lo_up",), 0, -1, lo_peer, 0, 4)
        to_core(0, -1)
        arrived(one_item, "down")
        pass_item(("far",), 0, 1, y_peer[-1], 4, 4)
        pass_item(("lo_down",), 0, 1, lo_peer, 0, 4)
        to_core(0, 1)

    def wo_3():
        arrived(one_item, "lo")
        pass_item(("lo_up",), 1, 0, y_peer[1], 4, 4)
        pass_item(("lo_down",), 1, 0, y_peer[-1], 4, 4)
        to_core(1, 0)

    def wo_4():
        arrived(one_item, "far")
        pass_item(("lo_far",), 0, 2, lo_peer, 0, 4)
        to_core(0, 2)
        arrived(one_item, "lo_up")
        pass_item(("lo_far",), 1, -1, y_peer[1], 4, 2)
        to_core(1, -1)
        arrived(one_item, "lo_down")
        pass_item(("lo_far",), 1, 1, y_peer[-1], 6, 2)
        to_core(1, 1)

    def wo_5():
        arrived(one_item, "lo_far")
        to_core(1, 2)

    def wo_6():
        arrived(wo.at[pl.ds(0, 4)], "core")

    def part_rows(piece):
        return WH_ROWS // (8 if KINDS[piece] == "Y" else 4)

    def part_start(piece, by):
        if KINDS[piece] == "Y":
            index = lax.rem(y + by + 4, 4) * 2 + core
        else:
            index = lax.rem(x_lo + by, 2) * 2 + core
        return index * part_rows(piece) + piece * WH_ROWS

    def piece_view(piece, by, low=0, size=None):
        size = part_rows(piece) if size is None else size
        return wh.at[pl.ds(pl.multiple_of(part_start(piece, by) + low, 16), size), pl.ds(NV, NV)]

    def wh_rows(count):
        return wh.at[pl.ds(0, count), pl.ds(0, NV)]

    def fetch_0(piece):
        by = 0 if KINDS[piece] == "Y" else 1
        rows = pl.ds(pl.multiple_of(part_start(piece, by), 16), part_rows(piece))
        move("wh", ("cut", piece), wh_ref.at[rows, :], piece_view(piece, by), cut_peer)

    def pass_part(key, view, peer):
        move("wh", key, view, view, peer)

    def fetch_1(piece):
        arrived(wh_rows(part_rows(piece)), "cut", piece)
        view = piece_view(piece, 0)
        if KINDS[piece] == "Y":
            pass_part(("next", piece), view, y_peer[1])
            pass_part(("next", piece), view, y_peer[-1])
        else:
            pass_part(("next", piece), view, lo_peer)
        pass_part(("wh_core",), view, sibling)

    def fetch_2(piece):
        size = part_rows(piece)
        if KINDS[piece] == "X":
            arrived(wh_rows(size), "next", piece)
            pass_part(("wh_core",), piece_view(piece, 1), sibling)
            return
        half = size // 2
        arrived(wh_rows(2 * size), "next", piece)
        pass_part(("second", piece), piece_view(piece, -1, 0, half), y_peer[1])
        pass_part(("second", piece), piece_view(piece, 1, half, half), y_peer[-1])
        pass_part(("wh_core",), piece_view(piece, -1), sibling)
        pass_part(("wh_core",), piece_view(piece, 1), sibling)

    def fetch_3(piece):
        arrived(wh_rows(part_rows(piece)), "second", piece)
        pass_part(("wh_core",), piece_view(piece, 2), sibling)

    def fetch_4():
        arrived(wh_rows(WH_ROWS // 2 * len(KINDS)), "wh_core")

    for copy in small:
        copy.wait()

    lane = lax.broadcasted_iota(jnp.int32, (8, TOK), 1)
    running = jnp.concatenate([ld_ref[...], jnp.zeros((6, TOK), F32)], axis=0)
    shift = 1
    while shift < TOK:
        running = running + jnp.where(lane >= shift, pltpu.roll(running, shift, axis=1), 0.0)
        shift *= 2
    seg_row = seg_ref[...].astype(F32)
    table = jnp.concatenate(
        [running[0:2], seg_row, tgt_ref[...].astype(F32), jnp.zeros((124, TOK), F32)], axis=0
    )
    columns[...] = table.T
    seg_col = columns[:, 2:3]
    seg_last = seg_col[TOK - 1 : TOK, :]

    decay = []
    own_state = []
    for h in range(2):
        head = slice(h * HD, (h + 1) * HD)
        cum_col = columns[:, h : h + 1]
        last = cum_col[TOK - 1 : TOK, :]
        tail = jnp.where(seg_col == seg_last, jnp.exp(last - cum_col), 0.0)
        weighted = (k_ref[:, head].astype(F32) * tail).astype(BF16)
        summary = lax.dot_general(
            weighted, v_ref[:, head], (((0,), (0,)), ((), ())), preferred_element_type=F32
        )
        own_state.append(summary)
        decay.append(jnp.exp(last))

    def pack(slot, states, decays, seg):
        for h in range(2):
            state_out[slot, h * HD : (h + 1) * HD, :] = states[h].astype(BF16)
        row = lax.broadcasted_iota(jnp.int32, (16, HD), 0)
        tops = [d.astype(BF16).astype(F32) for d in decays]
        block = jnp.where(row == 0, tops[0], 0.0)
        block = jnp.where(row == 1, decays[0] - tops[0], block)
        block = jnp.where(row == 2, tops[1], block)
        block = jnp.where(row == 3, decays[1] - tops[1], block)
        block = jnp.where(row == 4, seg, block)
        state_out[slot, 2 * HD : 2 * HD + 16, :] = block.astype(BF16)

    def unpack(buffer, slot):
        states = [buffer[slot, h * HD : (h + 1) * HD, :].astype(F32) for h in range(2)]
        block = buffer[slot, 2 * HD : 2 * HD + 16, :].astype(F32)
        decays = [block[0:1, 0:1] + block[1:2, 0:1], block[2:3, 0:1] + block[3:4, 0:1]]
        return states, decays, block[4:5, 0:1]

    def join(first, second):
        states = [
            jnp.where(first[2] == second[2], second[1][h], 0.0) * first[0][h] + second[0][h]
            for h in range(2)
        ]
        return states, [first[1][h] * second[1][h] for h in range(2)], second[2]

    def choose(flag, a, b):
        return (
            [jnp.where(flag, a[0][h], b[0][h]) for h in range(2)],
            [jnp.where(flag, a[1][h], b[1][h]) for h in range(2)],
            jnp.where(flag, a[2], b[2]),
        )

    pack(0, own_state, decay, seg_last)
    pl.semaphore_wait(barrier, len(peers))
    move("state", ("state_core",), state_out.at[0], state_in.at[0], sibling)
    own_strip_copy = wo_0()
    for by in OTHERS:
        cols = pl.ds(pl.multiple_of(along_z(by) * DZ, 128), DZ)
        move("res", ("res",), res_hbm.at[:, cols], res.at[z], z_peer[by])
    for piece in range(len(KINDS)):
        fetch_0(piece)
    cols = pl.ds(pl.multiple_of(z * DZ, 128), DZ)
    own_res = load(7, res_hbm.at[:, cols], res.at[z])
    load_gain = load(8, gain_hbm.at[:, cols], gain_ref)

    def inside(h):
        head = slice(h * HD, (h + 1) * HD)
        cum_col = columns[:, h : h + 1]
        cum_row = running[h : h + 1, :]
        for low in (0, 256):
            high = low + 256
            scores = lax.dot_general(
                q_ref[low:high, head], k_ref[0:high, head], (((1,), (1,)), ((), ())),
                preferred_element_type=F32,
            )
            at_row = lax.broadcasted_iota(jnp.int32, (256, high), 0) + low
            at_col = lax.broadcasted_iota(jnp.int32, (256, high), 1)
            allowed = (at_row >= at_col) & (seg_col[low:high] == seg_row[:, 0:high])
            spread = cum_col[low:high] - cum_row[:, 0:high]
            weights = jnp.exp(jnp.where(allowed, spread, -1e30))
            mixing = (scores * weights).astype(BF16)
            within[h, low:high, :] = dot(mixing, v_ref[0:high, head])

    arrived(state_in.at[0], "state_core")
    own_wh = load(9, wh_ref, wh.at[:, pl.ds(0, NV)])

    own = (own_state, decay, seg_last)
    other = unpack(state_in, 0)
    first = choose(core == 0, own, other)
    second = choose(core == 0, other, own)
    chip = join(first, second)
    pack(1, *chip)
    for index, by in enumerate((-1, 1, 2)):
        move("state", ("state_y",), state_out.at[1], state_in.at[1 + index], y_peer[by])
    load_q.wait()
    inside(0)
    inside(1)
    arrived(state_in.at[pl.ds(1, 3)], "state_y")
    chips = {0: chip}
    for index, by in enumerate((1, -1, 2)):
        chips[by] = unpack(state_in, 1 + index)

    def chip_at(target):
        picked = chips[0]
        for by in (1, -1, 2):
            picked = choose(lax.rem(y + by + 4, 4) == target, chips[by], picked)
        return picked

    nothing = ([jnp.zeros((HD, HD), F32)] * 2, [jnp.ones((1, 1), F32)] * 2, jnp.zeros((1, 1), F32))
    total = chip_at(0)
    before = choose(y == 0, nothing, total)
    for target in range(1, 4):
        total = join(total, chip_at(target))
        before = choose(y > target, total, before)
    pack(2, *total)
    move("state", ("total",), state_out.at[2], state_in.at[4], lo_peer)
    wo_1()
    arrived(state_in.at[4], "total")
    earlier = unpack(state_in, 4)
    joined = choose(y == 0, earlier, join(earlier, before))
    before = choose(x_lo == 0, before, joined)
    fresh = (x_lo == 0) & (y == 0)
    with_first = choose(fresh, first, join(before, first))
    before = choose(core == 0, before, with_first)
    prior = before[2]


    def own_heads(sub):
        return attn.at[x_hi if sub % 2 else 1 - x_hi, pl.ds(sub // 2 * 128, 128)]

    def wait_heads(step, key):
        arrived(heads.at[0, pl.ds(0, 2)], "heads", step, key)

    def send_heads(way, step, sub, key):
        src = own_heads(sub) if step == 0 else heads.at[GATHER_FROM[way][step], sub]
        dst = heads.at[GATHER_TO[way][step], sub]
        move("heads", ("heads", step, key), src, dst, z_peer[1 if way == 0 else -1])

    def gather_heads(step, sub):
        if step > 0:
            wait_heads(step - 1, sub)
        for way in range(2):
            send_heads(way, step, sub, sub)

    def last_heads(wave):
        for way in range(2):
            wait_heads(2, 2 * wave + way)
            send_heads(way, 3, 2 * wave + way, wave)

    for h in range(2):
        head = slice(h * HD, (h + 1) * HD)
        scale = jnp.where(seg_col == prior, jnp.exp(columns[:, h : h + 1]), 0.0)
        carried = dot(q_ref[:, head], before[0][h].astype(BF16))
        output = within[h] + scale * carried
        mean = jnp.mean(output * output, axis=-1, keepdims=True)
        scaled = (output * lax.rsqrt(mean + EPSILON)).astype(BF16)
        for j in range(NZ):
            for half in range(2):
                low = (2 * j + half) * CH
                attn[half, j * CH : (j + 1) * CH, head] = scaled[low : low + CH]
    for sub in range(3):
        gather_heads(0, sub)
    wo_2()
    wo_3()
    for j in range(NZ):
        rows = pl.ds(pl.multiple_of((2 * j + x_hi) * CH, CH), CH)
        goals[j * CH : (j + 1) * CH, :] = columns[rows, :]
    gather_heads(1, 0)
    gather_heads(1, 1)
    gather_heads(0, 3)
    gather_heads(2, 0)
    gather_heads(2, 1)
    wo_4()
    gather_heads(1, 2)
    fetch_1(0)
    wo_5()
    last_heads(0)
    gather_heads(1, 3)
    fetch_1(1)
    fetch_1(2)
    gather_heads(2, 2)
    wo_6()

    def project(slot, wave):
        if slot == 0:
            left = jnp.concatenate([own_heads(2 * wave + i)[...] for i in range(2)], axis=0)
        else:
            left = heads[slot, 2 * wave : 2 * wave + 2].reshape(HALF, HALF)
        return dot(left, wo[along_z(SLOT_OFFSET[slot])].reshape(HALF, DZ))

    def accumulate(wave, *slots):
        value = partial[wave]
        for slot in slots:
            value = value + project(slot, wave)
        partial[wave] = value

    def swap(wave):
        total = partial[wave] + project(7, wave)
        for i in range(2):
            sub = 2 * wave + i
            swap_out[sub * 64 : sub * 64 + 64, :] = total[i * 64 : i * 64 + 64].astype(BF16)
            view = pl.ds(sub * 64, 64)
            move("swap", ("swap", sub), swap_out.at[view], swap_in.at[view], hi_peer)
        stay = res[4 * wave : 4 * wave + 4].reshape(128, DZ).astype(F32)
        hidden[wave * 128 : wave * 128 + 128, :] = total[128:] + stay

    partial[0] = project(0, 0) + project(1, 0) + project(2, 0)
    accumulate(0, 3, 4)
    accumulate(0, 5, 6)
    own_res.wait()
    load_gain.wait()
    arrived(res.at[pl.ds(0, NZ - 1)], "res")
    wait_heads(3, 0)
    swap(0)
    gather_heads(2, 3)
    partial[1] = project(0, 1) + project(1, 1) + project(2, 1)
    last_heads(1)
    fetch_1(3)
    fetch_1(4)
    fetch_1(5)
    accumulate(1, 3, 4)

    def sub_rows(sub):
        return pl.ds(sub * 64, 64)

    def wait_hidden(step, key):
        arrived(slices.at[0, pl.ds(0, 128)], "hidden", step, key)

    def send_hidden(way, step, sub, key):
        src = slices.at[GATHER_FROM[way][step], sub_rows(sub)]
        dst = slices.at[GATHER_TO[way][step], sub_rows(sub)]
        move("hidden", ("hidden", step, key), src, dst, z_peer[1 if way == 0 else -1])

    def gather_hidden(step, sub):
        if step > 0:
            wait_hidden(step - 1, sub)
        for way in range(2):
            send_hidden(way, step, sub, sub)

    def last_hidden(wave):
        for way in range(2):
            wait_hidden(2, 2 * wave + way)
            send_hidden(way, 3, 2 * wave + way, wave)

    def finish(sub):
        arrived(swap_in.at[pl.ds(0, 64)], "swap", sub)
        rows = slice(sub * 64, (sub + 1) * 64)
        value = hidden[rows, :] + swap_in[rows, :].astype(F32)
        hidden[rows, :] = value
        slices[0, rows, :] = (value * gain_ref[...]).astype(BF16)
        gather_hidden(0, sub)

    own_tiles = (slice(0, 256), slice(256, 512), slice(512, 640))
    other_tiles = (slice(640, 896), slice(896, 1152), slice(1152, 1280))
    all_tiles = tuple(slice(i * TILE, (i + 1) * TILE) for i in range(5))

    def multiply(slots, low, high, cols, more=True):
        value = logits[low:high, cols] if more else 0.0
        for slot in slots:
            deep = pl.ds(pl.multiple_of(along_z(SLOT_OFFSET[slot]) * DZ, DZ), DZ)
            value = value + dot(slices[slot, low:high, :], wh[deep, cols])
        logits[low:high, cols] = value

    finish(0)
    finish(1)
    accumulate(1, 5, 6)
    wait_heads(3, 1)
    swap(1)
    gather_hidden(1, 0)
    finish(2)
    gather_hidden(1, 1)
    finish(3)
    square = jnp.sum(hidden[...] * hidden[...], axis=1, keepdims=True)
    turned = jnp.broadcast_to(square, (HALF, HD)).T
    squares[0] = jnp.concatenate(
        [turned[0:1, 0:HD], turned[0:1, HD:HALF], jnp.zeros((6, HD), F32)], axis=0
    )
    for slot in range(1, NZ):
        offset = SLOT_OFFSET[slot]
        peer = z_peer[offset if slot == NZ - 1 else -offset]
        move("square", ("square",), squares.at[0], squares.at[slot], peer)

    own_offset = vocab * NV
    other_offset = (z * 2 + 1 - x_hi) * NV

    def summarize(low, high):
        size = high - low
        values = logits[low:high, :] * factor[low:high]
        top = jnp.max(values, axis=1, keepdims=True)
        mass = jnp.sum(jnp.exp(values - top), axis=1, keepdims=True)
        column = lax.broadcasted_iota(jnp.int32, (size, 2 * NV), 1)
        column = jnp.where(column < NV, column + own_offset, column - NV + other_offset)
        goal = goals[low:high, 3:4].astype(jnp.int32)
        hit = jnp.sum(jnp.where(column == goal, values, 0.0), axis=1, keepdims=True)
        lane_of = lax.broadcasted_iota(jnp.int32, (size, HD), 1)
        stats[low:high, :] = jnp.where(lane_of == 0, top, jnp.where(lane_of == 1, mass, hit))

    own_wh.wait()
    fetch_2(0)
    for tile in own_tiles:
        multiply((0,), 0, HALF, tile, False)
    gather_hidden(1, 2)
    fetch_2(1)
    fetch_2(2)
    gather_hidden(1, 3)
    fetch_2(3)
    for tile in own_tiles:
        multiply((1, 2), 0, HALF, tile)
    gather_hidden(2, 0)
    fetch_2(4)
    gather_hidden(2, 1)
    fetch_2(5)
    gather_hidden(2, 2)
    fetch_3(1)
    fetch_3(2)
    fetch_3(3)
    gather_hidden(2, 3)
    fetch_3(4)
    fetch_3(5)
    for tile in own_tiles:
        multiply((3, 4), 0, HALF, tile)
    last_hidden(0)
    fetch_4()
    for tile in other_tiles:
        multiply((0, 1, 2, 3, 4), 0, HALF, tile, False)
    last_hidden(1)
    total_square = squares[0]
    arrived(squares.at[pl.ds(0, NZ - 1)], "square")
    for slot in range(1, NZ):
        total_square = total_square + squares[slot]
    factor = lax.rsqrt(total_square / D + EPSILON)
    factor = jnp.concatenate([factor, jnp.zeros((HD - 8, HD), F32)], axis=0).T
    factor = jnp.concatenate([factor[:, 0:1], factor[:, 1:2]], axis=0)
    for tile in all_tiles:
        multiply((5, 6), 0, HALF, tile)
    for i in range(2):
        wait_hidden(3, i)
        for tile in all_tiles:
            multiply((7,), i * 128, i * 128 + 128, tile)
        summarize(i * 128, i * 128 + 128)
    turned = stats[...].T
    for half in range(2):
        stats_out[half] = turned[0:8, half * HD : (half + 1) * HD]
    for by in (4, 3, -3, 2, -2, 1, -1):
        move("stats", ("stats",), stats_out.at[along_z(by) // 4], stats_in.at[by + 3], z_peer[by])
    blocks = [stats_out[z // 4]]
    arrived(stats_in.at[pl.ds(0, NZ - 1)], "stats")
    for by in OTHERS:
        blocks.append(stats_in[by + 3])
    top = blocks[0][0:1]
    for block in blocks[1:]:
        top = jnp.maximum(top, block[0:1])
    mass = jnp.zeros((1, HD), F32)
    hit = jnp.zeros((1, HD), F32)
    for block in blocks:
        mass = mass + block[1:2] * jnp.exp(block[0:1] - top)
        hit = hit + block[2:3]
    result = hit - top - jnp.log(mass)
    quarter = lax.rem(z, 4)
    picked = result[:, 0:CH]
    for i in range(1, 4):
        picked = jnp.where(quarter == i, result[:, i * CH : (i + 1) * CH], picked)
    out_ref[...] = picked
    departed(state_in, "state")
    departed(res.at[pl.ds(0, NZ - 1)], "res")
    departed(wo.at[0, pl.ds(0, 15)], "strip")
    departed(wo.at[pl.ds(0, NZ - 1)], "wo")
    departed(wh_rows(D), "wh")
    departed(heads.at[pl.ds(0, NZ - 1)], "heads")
    departed(swap_out, "swap")
    departed(slices.at[pl.ds(0, NZ - 1)], "hidden")
    departed(squares.at[pl.ds(0, NZ - 1)], "square")
    departed(stats_in.at[pl.ds(0, NZ - 1)], "stats")


def shards(
    query_rows, key_rows, value_rows, log_decay, segment_ids, residual, out_weight, final_gain,
    head_weight, targets,
):
    vmem = pl.BlockSpec(memory_space=pltpu.VMEM)
    hbm = pl.BlockSpec(memory_space=pl.ANY)
    dma = pltpu.SemaphoreType.DMA
    result = pl.pallas_call(
        kernel,
        out_shape=jax.ShapeDtypeStruct((1, CH), F32),
        in_specs=[hbm] * 10,
        out_specs=vmem,
        scratch_shapes=[
            pltpu.VMEM((TOK, 2 * HD), BF16),
            pltpu.VMEM((TOK, 2 * HD), BF16),
            pltpu.VMEM((TOK, 2 * HD), BF16),
            pltpu.VMEM((2, TOK), F32),
            pltpu.VMEM((1, TOK), jnp.int32),
            pltpu.VMEM((1, TOK), jnp.int32),
            pltpu.VMEM((NZ, CH, DZ), BF16),
            pltpu.VMEM((1, DZ), F32),
            pltpu.VMEM((NZ, 16, 16, DZ), BF16),
            pltpu.VMEM((D, 2 * NV), BF16),
            pltpu.VMEM((2, HALF, 2 * HD), BF16),
            pltpu.VMEM((NZ, 4, 128, 2 * HD), BF16),
            pltpu.VMEM((2, HALF, DZ), F32),
            pltpu.VMEM((HALF, DZ), F32),
            pltpu.VMEM((HALF, DZ), BF16),
            pltpu.VMEM((HALF, DZ), BF16),
            pltpu.VMEM((NZ, HALF, DZ), BF16),
            pltpu.VMEM((HALF, 2 * NV), F32),
            pltpu.VMEM((NZ, 8, HD), F32),
            pltpu.VMEM((2, TOK, HD), F32),
            pltpu.VMEM((TOK, HD), F32),
            pltpu.VMEM((HALF, HD), F32),
            pltpu.VMEM((3, 2 * HD + 16, HD), BF16),
            pltpu.VMEM((5, 2 * HD + 16, HD), BF16),
            pltpu.VMEM((HALF, HD), F32),
            pltpu.VMEM((2, 8, HD), F32),
            pltpu.VMEM((NZ, 8, HD), F32),
            dma((10,)),
            dma((len(GROUPS),)),
            dma((ARRIVALS,)),
        ],
        compiler_params=pltpu.CompilerParams(
            collective_id=0, has_side_effects=True, vmem_limit_bytes=56 * 1024 * 1024
        ),
        name="layer",
    )(
        query_rows, key_rows, value_rows, log_decay, segment_ids.reshape(1, -1),
        targets.reshape(1, -1), residual, final_gain.reshape(1, -1), out_weight, head_weight,
    )
    return result.reshape(CH)


def solution(mesh):
    in_specs = (
        P("ctx", "vocab"),
        P("ctx", "vocab"),
        P("ctx", "vocab"),
        P("vocab", "ctx"),
        P("ctx"),
        P(("ctx", "vocab"), None),
        P("vocab", None),
        P(),
        P(None, "vocab"),
        P("ctx"),
    )
    out_specs = P(("ctx", "vocab"))
    return jax.shard_map(shards, mesh=mesh, in_specs=in_specs, out_specs=out_specs, check_vma=False)
```

```python
import jax
import jax.numpy as jnp
from jax import lax
from jax.experimental import pallas as pl
from jax.experimental.pallas import tpu as pltpu
from jax.sharding import PartitionSpec as P

EPSILON = 1e-06
MESH = pl.DeviceIdType.MESH
F32 = jnp.float32
BF16 = jnp.bfloat16

TOK = 512
D = 6144
HD = 128
NV = 640
CH = 32
NZ = 8
HALF = 256
DZ = 768
TILE = 256
ARRIVALS = 65
GROUPS = ("state", "res", "strip", "wo", "wh", "heads", "swap", "hidden", "square", "stats")

STATE = 144
CHIPS = ((0, -1), (0, 1), (0, 2), (1, 0), (1, -1), (1, 1), (1, 2))
OTHERS = (1, -1, 2, -2, 3, -3, 4)
EARLY = 6
SLOT_OFFSET = (0, -1, 1, -2, 2, -3, 3, 4)
GATHER_FROM = ((0, 1, 3, 5), (0, 2, 4, 6))
GATHER_TO = ((1, 3, 5, 7), (2, 4, 6, 7))

KINDS = "XYYYYY"
WH_ROWS = 1024


def dot(a, b):
    return jnp.dot(a, b, preferred_element_type=F32)


def kernel(
    q_hbm, k_hbm, v_hbm, ld_hbm, seg_hbm, tgt_hbm, res_hbm, gain_hbm, wo_ref, wh_ref,
    out_ref,
    q_ref, k_ref, v_ref, ld_ref, seg_ref, tgt_ref, res, gain_ref,
    wo, wh, attn, heads, partial, hidden, swap_out, swap_in, slices, logits, squares, within, columns, goals,
    state_out, state_in, stats, stats_out, stats_in,
    local_sem, send_sem, recv_sem,
):
    ctx = lax.axis_index("ctx")
    vocab = lax.axis_index("vocab")
    x_lo = ctx // 8
    y = lax.rem(ctx // 2, 4)
    core = lax.rem(ctx, 2)
    z = vocab // 2
    x_hi = lax.rem(vocab, 2)

    def at_y(by):
        return x_lo * 8 + lax.rem(y + by + 4, 4) * 2 + core

    def along_z(by):
        return lax.rem(z + by + NZ, NZ)

    sibling = (ctx + 1 - 2 * core, vocab)
    y_peer = {by: (at_y(by), vocab) for by in (-1, 1, 2)}
    lo_peer = (lax.rem(ctx + 8, 16), vocab)
    chip_peer = {
        (lo, by): (lax.rem(x_lo + lo, 2) * 8 + lax.rem(y + by + 4, 4) * 2 + core, vocab)
        for lo, by in CHIPS
    }
    cut_peer = (lax.rem(ctx + 8, 16), z * 2 + 1 - x_hi)
    hi_peer = (ctx, z * 2 + 1 - x_hi)
    z_peer = {by: (ctx, along_z(by) * 2 + x_hi) for by in (-3, -2, -1, 1, 2, 3, 4)}

    barrier = pltpu.get_barrier_semaphore()
    peers = [sibling, cut_peer, hi_peer, *chip_peer.values(), *z_peer.values()]
    for peer in peers:
        pl.semaphore_signal(barrier, inc=1, device_id=peer, device_id_type=MESH)

    def load(index, src, dst):
        copy = pltpu.make_async_copy(src, dst, local_sem.at[index])
        copy.start()
        return copy

    small = [
        load(0, ld_hbm, ld_ref), load(1, seg_hbm, seg_ref), load(2, tgt_hbm, tgt_ref),
        load(3, k_hbm, k_ref), load(4, v_hbm, v_ref),
    ]
    load_q = load(5, q_hbm, q_ref)

    arrivals = {}

    def move(group, key, src, dst, peer):
        index = arrivals.setdefault(key, len(arrivals))
        pltpu.make_async_remote_copy(
            src_ref=src, dst_ref=dst, send_sem=send_sem.at[GROUPS.index(group)],
            recv_sem=recv_sem.at[index], device_id=peer, device_id_type=MESH,
        ).start()

    def arrived(like, *key):
        pltpu.make_async_copy(like, like, recv_sem.at[arrivals[key]]).wait()

    def departed(like, group):
        pltpu.make_async_copy(like, like, send_sem.at[GROUPS.index(group)]).wait()

    def strip(at_lo, at_row, of_core):
        return of_core * 8 + at_lo * 4 + at_row

    def item(lo, by, first=0, count=NZ):
        row = lax.rem(y + by + 4, 4)
        return wo.at[pl.ds(first, count), strip(lax.rem(x_lo + lo, 2), row, core)]

    own_strip = strip(x_lo, y, core)

    def pass_item(key, lo, by, peer, first=0, count=NZ):
        view = item(lo, by, first, count)
        move("wo", key, view, view, peer)

    def wo_0():
        rows = pl.ds(pl.multiple_of(own_strip * 16, 16), 16)
        for by in OTHERS:
            cols = pl.ds(pl.multiple_of(along_z(by) * DZ, 128), DZ)
            move("strip", ("z",), wo_ref.at[rows, cols], wo.at[z, own_strip], z_peer[by])
        cols = pl.ds(pl.multiple_of(z * DZ, 128), DZ)
        return load(6, wo_ref.at[rows, cols], wo.at[z, own_strip])

    one_item = wo.at[0, pl.ds(0, 8)]

    def to_core(lo, by):
        view = item(lo, by)
        move("strip" if (lo, by) == (0, 0) else "wo", ("core",), view, view, sibling)

    def wo_1():
        arrived(wo.at[0, pl.ds(0, NZ - 1)], "z")
        own_strip_copy.wait()
        pass_item(("up",), 0, 0, y_peer[1])
        pass_item(("down",), 0, 0, y_peer[-1])
        pass_item(("lo",), 0, 0, lo_peer)
        to_core(0, 0)

    def wo_2():
        arrived(one_item, "up")
        pass_item(("far",), 0, -1, y_peer[1], 0, 4)
        pass_item(("lo_up",), 0, -1, lo_peer, 0, 4)
        to_core(0, -1)
        arrived(one_item, "down")
        pass_item(("far",), 0, 1, y_peer[-1], 4, 4)
        pass_item(("lo_down",), 0, 1, lo_peer, 0, 4)
        to_core(0, 1)

    def wo_3():
        arrived(one_item, "lo")
        pass_item(("lo_up",), 1, 0, y_peer[1], 4, 4)
        pass_item(("lo_down",), 1, 0, y_peer[-1], 4, 4)
        to_core(1, 0)

    def wo_4():
        arrived(one_item, "far")
        pass_item(("lo_far",), 0, 2, lo_peer, 0, 4)
        to_core(0, 2)
        arrived(one_item, "lo_up")
        pass_item(("lo_far",), 1, -1, y_peer[1], 4, 2)
        to_core(1, -1)
        arrived(one_item, "lo_down")
        pass_item(("lo_far",), 1, 1, y_peer[-1], 6, 2)
        to_core(1, 1)

    def wo_5():
        arrived(one_item, "lo_far")
        to_core(1, 2)

    def wo_6():
        arrived(wo.at[pl.ds(0, 4)], "core")

    def part_rows(piece):
        return WH_ROWS // (8 if KINDS[piece] == "Y" else 4)

    def part_start(piece, by):
        if KINDS[piece] == "Y":
            index = lax.rem(y + by + 4, 4) * 2 + core
        else:
            index = lax.rem(x_lo + by, 2) * 2 + core
        return index * part_rows(piece) + piece * WH_ROWS

    def piece_view(piece, by, low=0, size=None):
        size = part_rows(piece) if size is None else size
        return wh.at[pl.ds(pl.multiple_of(part_start(piece, by) + low, 16), size), pl.ds(NV, NV)]

    def wh_rows(count):
        return wh.at[pl.ds(0, count), pl.ds(0, NV)]

    def fetch_0(piece):
        by = 0 if KINDS[piece] == "Y" else 1
        rows = pl.ds(pl.multiple_of(part_start(piece, by), 16), part_rows(piece))
        move("wh", ("cut", piece), wh_ref.at[rows, :], piece_view(piece, by), cut_peer)

    def pass_part(key, view, peer):
        move("wh", key, view, view, peer)

    def fetch_1(piece):
        arrived(wh_rows(part_rows(piece)), "cut", piece)
        view = piece_view(piece, 0)
        if KINDS[piece] == "Y":
            pass_part(("next", piece), view, y_peer[1])
            pass_part(("next", piece), view, y_peer[-1])
        else:
            pass_part(("next", piece), view, lo_peer)
        pass_part(("wh_core",), view, sibling)

    def fetch_2(piece):
        size = part_rows(piece)
        if KINDS[piece] == "X":
            arrived(wh_rows(size), "next", piece)
            pass_part(("wh_core",), piece_view(piece, 1), sibling)
            return
        half = size // 2
        arrived(wh_rows(2 * size), "next", piece)
        pass_part(("second", piece), piece_view(piece, -1, 0, half), y_peer[1])
        pass_part(("second", piece), piece_view(piece, 1, half, half), y_peer[-1])
        pass_part(("wh_core",), piece_view(piece, -1), sibling)
        pass_part(("wh_core",), piece_view(piece, 1), sibling)

    def fetch_3(piece):
        arrived(wh_rows(part_rows(piece)), "second", piece)
        pass_part(("wh_core",), piece_view(piece, 2), sibling)

    def fetch_4():
        arrived(wh_rows(WH_ROWS // 2 * len(KINDS)), "wh_core")

    for copy in small:
        copy.wait()

    lane = lax.broadcasted_iota(jnp.int32, (8, TOK), 1)
    running = jnp.concatenate([ld_ref[...], jnp.zeros((6, TOK), F32)], axis=0)
    shift = 1
    while shift < TOK:
        running = running + jnp.where(lane >= shift, pltpu.roll(running, shift, axis=1), 0.0)
        shift *= 2
    seg_row = seg_ref[...].astype(F32)
    table = jnp.concatenate(
        [running[0:2], seg_row, tgt_ref[...].astype(F32), jnp.zeros((124, TOK), F32)], axis=0
    )
    columns[...] = table.T
    seg_col = columns[:, 2:3]
    seg_last = seg_col[TOK - 1 : TOK, :]

    decay = []
    own_state = []
    for h in range(2):
        head = slice(h * HD, (h + 1) * HD)
        cum_col = columns[:, h : h + 1]
        last = cum_col[TOK - 1 : TOK, :]
        tail = jnp.where(seg_col == seg_last, jnp.exp(last - cum_col), 0.0)
        weighted = (k_ref[:, head].astype(F32) * tail).astype(BF16)
        summary = lax.dot_general(
            weighted, v_ref[:, head], (((0,), (0,)), ((), ())), preferred_element_type=F32
        )
        own_state.append(summary)
        decay.append(jnp.exp(last))

    def pack(start, state, falloff, seg):
        state_out[start : start + HD, :] = state.astype(BF16)
        row = lax.broadcasted_iota(jnp.int32, (16, HD), 0)
        high = falloff.astype(BF16).astype(F32)
        block = jnp.where(row == 0, high, jnp.where(row == 1, falloff - high, 0.0))
        block = jnp.where(row == 2, seg, block)
        state_out[start + HD : start + STATE, :] = block.astype(BF16)

    def unpack(start):
        block = state_in[start + HD : start + STATE, :].astype(F32)
        return (
            state_in[start : start + HD, :].astype(F32),
            block[0:1, 0:1] + block[1:2, 0:1],
            block[2:3, 0:1],
        )

    def join(first, second):
        state = jnp.where(first[2] == second[2], second[1], 0.0) * first[0] + second[0]
        return state, first[1] * second[1], second[2]

    def choose(flag, a, b):
        return tuple(jnp.where(flag, one, other) for one, other in zip(a, b))

    def of_head(h):
        return own_state[h], decay[h], seg_last

    pack(0, *choose(core == 0, of_head(1), of_head(0)))
    def send_res(offsets):
        for by in offsets:
            cols = pl.ds(pl.multiple_of(along_z(by) * DZ, 128), DZ)
            move("res", ("res",), res_hbm.at[:, cols], res.at[z], z_peer[by])

    pl.semaphore_wait(barrier, len(peers))
    rows = pl.ds(0, STATE)
    move("state", ("state_core",), state_out.at[rows], state_in.at[rows], sibling)
    own_strip_copy = wo_0()
    send_res(OTHERS[:EARLY])
    for piece in range(len(KINDS)):
        fetch_0(piece)
    cols = pl.ds(pl.multiple_of(z * DZ, 128), DZ)
    own_res = load(7, res_hbm.at[:, cols], res.at[z])
    load_gain = load(8, gain_hbm.at[:, cols], gain_ref)

    def inside(h):
        head = slice(h * HD, (h + 1) * HD)
        cum_col = columns[:, h : h + 1]
        cum_row = running[h : h + 1, :]
        for low in (0, 256):
            high = low + 256
            scores = lax.dot_general(
                q_ref[low:high, head], k_ref[0:high, head], (((1,), (1,)), ((), ())),
                preferred_element_type=F32,
            )
            at_row = lax.broadcasted_iota(jnp.int32, (256, high), 0) + low
            at_col = lax.broadcasted_iota(jnp.int32, (256, high), 1)
            allowed = (at_row >= at_col) & (seg_col[low:high] == seg_row[:, 0:high])
            spread = cum_col[low:high] - cum_row[:, 0:high]
            weights = jnp.exp(jnp.where(allowed, spread, -1e30))
            mixing = (scores * weights).astype(BF16)
            within[h, low:high, :] = dot(mixing, v_ref[0:high, head])

    arrived(state_in.at[pl.ds(0, STATE)], "state_core")
    own_wh = load(9, wh_ref, wh.at[:, pl.ds(0, NV)])
    own = choose(core == 0, of_head(0), of_head(1))
    other = unpack(0)
    first = choose(core == 0, own, other)
    second = choose(core == 0, other, own)
    chip = join(first, second)
    pack(STATE, *chip)
    for index, peer in enumerate(CHIPS):
        src = state_out.at[pl.ds(STATE, STATE)]
        dst = state_in.at[pl.ds((1 + index) * STATE, STATE)]
        move("state", ("chips",), src, dst, chip_peer[peer])
    load_q.wait()
    inside(0)
    inside(1)
    arrived(state_in.at[pl.ds(STATE, len(CHIPS) * STATE)], "chips")
    chips = {(0, 0): chip}
    for index, (lo, by) in enumerate(CHIPS):
        chips[lo, by if by in (0, 2) else -by] = unpack((1 + index) * STATE)

    def chip_at(target):
        picked = chip
        for (lo, by), value in chips.items():
            if (lo, by) != (0, 0):
                number = lax.rem(x_lo + lo, 2) * 4 + lax.rem(y + by + 4, 4)
                picked = choose(number == target, value, picked)
        return picked

    my_chip = x_lo * 4 + y
    total = chip_at(0)
    before = choose(my_chip == 0, (jnp.zeros((HD, HD), F32),) + chip[1:], total)
    for target in range(1, 7):
        total = join(total, chip_at(target))
        before = choose(my_chip > target, total, before)
    inner = choose(my_chip == 0, first, join(before, first))
    mine = choose(core == 0, before, inner)
    others = choose(core == 0, inner, before)
    prior = mine[2]
    state_out[2 * STATE : 2 * STATE + HD, :] = others[0].astype(BF16)
    last_rows = pl.ds(8 * STATE, HD)
    move(
        "state", ("incoming",), state_out.at[pl.ds(2 * STATE, HD)], state_in.at[last_rows], sibling
    )
    wo_1()
    arrived(state_in.at[last_rows], "incoming")
    received = state_in[8 * STATE : 8 * STATE + HD, :].astype(F32)
    incoming = [jnp.where(core == h, mine[0], received).astype(BF16) for h in range(2)]

    def own_heads(sub):
        return attn.at[x_hi if sub % 2 else 1 - x_hi, pl.ds(sub // 2 * 128, 128)]

    def wait_heads(step, key):
        arrived(heads.at[0, pl.ds(0, 2)], "heads", step, key)

    def send_heads(way, step, sub, key):
        src = own_heads(sub) if step == 0 else heads.at[GATHER_FROM[way][step], sub]
        dst = heads.at[GATHER_TO[way][step], sub]
        move("heads", ("heads", step, key), src, dst, z_peer[1 if way == 0 else -1])

    def gather_heads(step, sub):
        if step > 0:
            wait_heads(step - 1, sub)
        for way in range(2):
            send_heads(way, step, sub, sub)

    def last_heads(wave):
        for way in range(2):
            wait_heads(2, 2 * wave + way)
            send_heads(way, 3, 2 * wave + way, wave)

    for h in range(2):
        head = slice(h * HD, (h + 1) * HD)
        scale = jnp.where(seg_col == prior, jnp.exp(columns[:, h : h + 1]), 0.0)
        carried = dot(q_ref[:, head], incoming[h])
        output = within[h] + scale * carried
        mean = jnp.mean(output * output, axis=-1, keepdims=True)
        scaled = (output * lax.rsqrt(mean + EPSILON)).astype(BF16)
        for j in range(NZ):
            for half in range(2):
                low = (2 * j + half) * CH
                attn[half, j * CH : (j + 1) * CH, head] = scaled[low : low + CH]
    for sub in range(2):
        gather_heads(0, sub)
    gather_heads(1, 0)
    gather_heads(1, 1)
    gather_heads(0, 2)
    wo_2()
    wo_3()
    for j in range(NZ):
        rows = pl.ds(pl.multiple_of((2 * j + x_hi) * CH, CH), CH)
        goals[j * CH : (j + 1) * CH, :] = columns[rows, :]
    gather_heads(2, 0)
    gather_heads(0, 3)
    gather_heads(2, 1)
    gather_heads(1, 2)
    wo_4()
    fetch_1(0)
    gather_heads(1, 3)
    last_heads(0)
    wo_5()
    gather_heads(2, 2)
    fetch_1(1)
    fetch_1(2)
    wo_6()

    def project(slot, wave):
        if slot == 0:
            left = jnp.concatenate([own_heads(2 * wave + i)[...] for i in range(2)], axis=0)
        else:
            left = heads[slot, 2 * wave : 2 * wave + 2].reshape(HALF, HALF)
        return dot(left, wo[along_z(SLOT_OFFSET[slot])].reshape(HALF, DZ))

    def accumulate(wave, *slots):
        value = partial[wave]
        for slot in slots:
            value = value + project(slot, wave)
        partial[wave] = value

    def swap(wave):
        total = partial[wave] + project(7, wave)
        for i in range(2):
            sub = 2 * wave + i
            swap_out[sub * 64 : sub * 64 + 64, :] = total[i * 64 : i * 64 + 64].astype(BF16)
            view = pl.ds(sub * 64, 64)
            move("swap", ("swap", sub), swap_out.at[view], swap_in.at[view], hi_peer)
        hidden[wave * 128 : wave * 128 + 128, :] = total[128:]

    partial[0] = project(0, 0) + project(1, 0) + project(2, 0)
    accumulate(0, 3, 4)
    accumulate(0, 5, 6)
    gather_heads(2, 3)
    wait_heads(3, 0)
    swap(0)
    send_res(OTHERS[EARLY:])
    partial[1] = project(0, 1) + project(1, 1) + project(2, 1)
    last_heads(1)
    fetch_1(3)
    fetch_1(4)
    fetch_1(5)
    accumulate(1, 3, 4)

    def sub_rows(sub):
        return pl.ds(sub * 64, 64)

    def wait_hidden(step, key):
        arrived(slices.at[0, pl.ds(0, 128)], "hidden", step, key)

    def send_hidden(way, step, sub, key):
        src = slices.at[GATHER_FROM[way][step], sub_rows(sub)]
        dst = slices.at[GATHER_TO[way][step], sub_rows(sub)]
        move("hidden", ("hidden", step, key), src, dst, z_peer[1 if way == 0 else -1])

    def gather_hidden(step, sub):
        if step > 0:
            wait_hidden(step - 1, sub)
        for way in range(2):
            send_hidden(way, step, sub, sub)

    def last_hidden(wave):
        for way in range(2):
            wait_hidden(2, 2 * wave + way)
            send_hidden(way, 3, 2 * wave + way, wave)

    def finish(sub):
        arrived(swap_in.at[pl.ds(0, 64)], "swap", sub)
        rows = slice(sub * 64, (sub + 1) * 64)
        value = hidden[rows, :] + swap_in[rows, :].astype(F32)
        value = value + res[2 * sub : 2 * sub + 2].reshape(64, DZ).astype(F32)
        hidden[rows, :] = value
        slices[0, rows, :] = (value * gain_ref[...]).astype(BF16)
        gather_hidden(0, sub)

    own_tiles = (slice(0, 256), slice(256, 512), slice(512, 640))
    other_tiles = (slice(640, 896), slice(896, 1152), slice(1152, 1280))
    all_tiles = tuple(slice(i * TILE, (i + 1) * TILE) for i in range(5))

    def multiply(slots, low, high, cols, more=True):
        value = logits[low:high, cols] if more else 0.0
        for slot in slots:
            deep = pl.ds(pl.multiple_of(along_z(SLOT_OFFSET[slot]) * DZ, DZ), DZ)
            value = value + dot(slices[slot, low:high, :], wh[deep, cols])
        logits[low:high, cols] = value

    own_res.wait()
    load_gain.wait()
    arrived(res.at[pl.ds(0, NZ - 1)], "res")
    finish(0)
    finish(1)
    accumulate(1, 5, 6)
    wait_heads(3, 1)
    swap(1)
    gather_hidden(1, 0)
    finish(2)
    gather_hidden(1, 1)
    finish(3)
    square = jnp.sum(hidden[...] * hidden[...], axis=1, keepdims=True)
    turned = jnp.broadcast_to(square, (HALF, HD)).T
    squares[0] = jnp.concatenate(
        [turned[0:1, 0:HD], turned[0:1, HD:HALF], jnp.zeros((6, HD), F32)], axis=0
    )
    for slot in range(1, NZ):
        offset = SLOT_OFFSET[slot]
        peer = z_peer[offset if slot == NZ - 1 else -offset]
        move("square", ("square",), squares.at[0], squares.at[slot], peer)

    own_offset = vocab * NV
    other_offset = (z * 2 + 1 - x_hi) * NV

    def summarize(low, high):
        size = high - low
        values = logits[low:high, :] * factor[low:high]
        top = jnp.max(values, axis=1, keepdims=True)
        mass = jnp.sum(jnp.exp(values - top), axis=1, keepdims=True)
        column = lax.broadcasted_iota(jnp.int32, (size, 2 * NV), 1)
        column = jnp.where(column < NV, column + own_offset, column - NV + other_offset)
        goal = goals[low:high, 3:4].astype(jnp.int32)
        hit = jnp.sum(jnp.where(column == goal, values, 0.0), axis=1, keepdims=True)
        lane_of = lax.broadcasted_iota(jnp.int32, (size, HD), 1)
        stats[low:high, :] = jnp.where(lane_of == 0, top, jnp.where(lane_of == 1, mass, hit))

    own_wh.wait()
    fetch_2(0)
    for tile in own_tiles:
        multiply((0,), 0, HALF, tile, False)
    gather_hidden(1, 2)
    fetch_2(1)
    fetch_2(2)
    gather_hidden(1, 3)
    fetch_2(3)
    for tile in own_tiles:
        multiply((1, 2), 0, HALF, tile)
    gather_hidden(2, 0)
    fetch_2(4)
    gather_hidden(2, 1)
    fetch_2(5)
    gather_hidden(2, 2)
    fetch_3(1)
    fetch_3(2)
    fetch_3(3)
    gather_hidden(2, 3)
    fetch_3(4)
    fetch_3(5)
    for tile in own_tiles:
        multiply((3, 4), 0, HALF, tile)
    last_hidden(0)
    fetch_4()
    for tile in other_tiles:
        multiply((0, 1, 2, 3, 4), 0, HALF, tile, False)
    last_hidden(1)
    total_square = squares[0]
    arrived(squares.at[pl.ds(0, NZ - 1)], "square")
    for slot in range(1, NZ):
        total_square = total_square + squares[slot]
    factor = lax.rsqrt(total_square / D + EPSILON)
    factor = jnp.concatenate([factor, jnp.zeros((HD - 8, HD), F32)], axis=0).T
    factor = jnp.concatenate([factor[:, 0:1], factor[:, 1:2]], axis=0)
    for tile in all_tiles:
        multiply((5, 6), 0, HALF, tile)
    for i in range(2):
        wait_hidden(3, i)
        for tile in all_tiles:
            multiply((7,), i * 128, i * 128 + 128, tile)
        summarize(i * 128, i * 128 + 128)
    turned = stats[...].T
    for half in range(2):
        stats_out[half] = turned[0:8, half * HD : (half + 1) * HD]
    for by in (4, 3, -3, 2, -2, 1, -1):
        move("stats", ("stats",), stats_out.at[along_z(by) // 4], stats_in.at[by + 3], z_peer[by])
    blocks = [stats_out[z // 4]]
    arrived(stats_in.at[pl.ds(0, NZ - 1)], "stats")
    for by in OTHERS:
        blocks.append(stats_in[by + 3])
    top = blocks[0][0:1]
    for block in blocks[1:]:
        top = jnp.maximum(top, block[0:1])
    mass = jnp.zeros((1, HD), F32)
    hit = jnp.zeros((1, HD), F32)
    for block in blocks:
        mass = mass + block[1:2] * jnp.exp(block[0:1] - top)
        hit = hit + block[2:3]
    result = hit - top - jnp.log(mass)
    quarter = lax.rem(z, 4)
    picked = result[:, 0:CH]
    for i in range(1, 4):
        picked = jnp.where(quarter == i, result[:, i * CH : (i + 1) * CH], picked)
    out_ref[...] = picked
    departed(state_in, "state")
    departed(res.at[pl.ds(0, NZ - 1)], "res")
    departed(wo.at[0, pl.ds(0, 15)], "strip")
    departed(wo.at[pl.ds(0, NZ - 1)], "wo")
    departed(wh_rows(D), "wh")
    departed(heads.at[pl.ds(0, NZ - 1)], "heads")
    departed(swap_out, "swap")
    departed(slices.at[pl.ds(0, NZ - 1)], "hidden")
    departed(squares.at[pl.ds(0, NZ - 1)], "square")
    departed(stats_in.at[pl.ds(0, NZ - 1)], "stats")


def shards(
    query_rows, key_rows, value_rows, log_decay, segment_ids, residual, out_weight, final_gain,
    head_weight, targets,
):
    vmem = pl.BlockSpec(memory_space=pltpu.VMEM)
    hbm = pl.BlockSpec(memory_space=pl.ANY)
    dma = pltpu.SemaphoreType.DMA
    result = pl.pallas_call(
        kernel,
        out_shape=jax.ShapeDtypeStruct((1, CH), F32),
        in_specs=[hbm] * 10,
        out_specs=vmem,
        scratch_shapes=[
            pltpu.VMEM((TOK, 2 * HD), BF16),
            pltpu.VMEM((TOK, 2 * HD), BF16),
            pltpu.VMEM((TOK, 2 * HD), BF16),
            pltpu.VMEM((2, TOK), F32),
            pltpu.VMEM((1, TOK), jnp.int32),
            pltpu.VMEM((1, TOK), jnp.int32),
            pltpu.VMEM((NZ, CH, DZ), BF16),
            pltpu.VMEM((1, DZ), F32),
            pltpu.VMEM((NZ, 16, 16, DZ), BF16),
            pltpu.VMEM((D, 2 * NV), BF16),
            pltpu.VMEM((2, HALF, 2 * HD), BF16),
            pltpu.VMEM((NZ, 4, 128, 2 * HD), BF16),
            pltpu.VMEM((2, HALF, DZ), F32),
            pltpu.VMEM((HALF, DZ), F32),
            pltpu.VMEM((HALF, DZ), BF16),
            pltpu.VMEM((HALF, DZ), BF16),
            pltpu.VMEM((NZ, HALF, DZ), BF16),
            pltpu.VMEM((HALF, 2 * NV), F32),
            pltpu.VMEM((NZ, 8, HD), F32),
            pltpu.VMEM((2, TOK, HD), F32),
            pltpu.VMEM((TOK, HD), F32),
            pltpu.VMEM((HALF, HD), F32),
            pltpu.VMEM((2 * STATE + HD, HD), BF16),
            pltpu.VMEM((8 * STATE + HD, HD), BF16),
            pltpu.VMEM((HALF, HD), F32),
            pltpu.VMEM((2, 8, HD), F32),
            pltpu.VMEM((NZ, 8, HD), F32),
            dma((10,)),
            dma((len(GROUPS),)),
            dma((ARRIVALS,)),
        ],
        compiler_params=pltpu.CompilerParams(
            collective_id=0, has_side_effects=True, vmem_limit_bytes=56 * 1024 * 1024
        ),
        name="layer",
    )(
        query_rows, key_rows, value_rows, log_decay, segment_ids.reshape(1, -1),
        targets.reshape(1, -1), residual, final_gain.reshape(1, -1), out_weight, head_weight,
    )
    return result.reshape(CH)


def solution(mesh):
    in_specs = (
        P("ctx", "vocab"),
        P("ctx", "vocab"),
        P("ctx", "vocab"),
        P("vocab", "ctx"),
        P("ctx"),
        P(("ctx", "vocab"), None),
        P("vocab", None),
        P(),
        P(None, "vocab"),
        P("ctx"),
    )
    out_specs = P(("ctx", "vocab"))
    return jax.shard_map(shards, mesh=mesh, in_specs=in_specs, out_specs=out_specs, check_vma=False)
```

```python
import jax
import jax.numpy as jnp
from jax import lax
from jax.experimental import pallas as pl
from jax.experimental.pallas import tpu as pltpu
from jax.sharding import PartitionSpec as P

EPSILON = 1e-06
MESH = pl.DeviceIdType.MESH
F32 = jnp.float32
BF16 = jnp.bfloat16

TOK = 512
D = 6144
HD = 128
NV = 640
CH = 32
NZ = 8
HALF = 256
DZ = 768
TILE = 256
ARRIVALS = 65
GROUPS = ("state", "res", "strip", "wo", "wh", "heads", "swap", "hidden", "square", "stats")

STATE = 144
CHIPS = ((0, -1), (0, 1), (0, 2), (1, 0), (1, -1), (1, 1), (1, 2))
OTHERS = (1, -1, 2, -2, 3, -3, 4)
EARLY = 6
SLOT_OFFSET = (0, -1, 1, -2, 2, -3, 3, 4)
GATHER_FROM = ((0, 1, 3, 5), (0, 2, 4, 6))
GATHER_TO = ((1, 3, 5, 7), (2, 4, 6, 7))

KINDS = "XYYYYY"
WH_ROWS = 1024


def dot(a, b):
    return jnp.dot(a, b, preferred_element_type=F32)


def kernel(
    q_hbm, k_hbm, v_hbm, ld_hbm, seg_hbm, tgt_hbm, res_hbm, gain_hbm, wo_ref, wh_ref,
    out_ref,
    q_ref, k_ref, v_ref, ld_ref, seg_ref, tgt_ref, res, gain_ref,
    wo, wh, attn, heads, partial, hidden, swap_out, swap_in, slices, logits, squares, within, columns, goals,
    state_out, state_in, stats, stats_out, stats_in,
    local_sem, send_sem, recv_sem,
):
    ctx = lax.axis_index("ctx")
    vocab = lax.axis_index("vocab")
    x_lo = ctx // 8
    y = lax.rem(ctx // 2, 4)
    core = lax.rem(ctx, 2)
    z = vocab // 2
    x_hi = lax.rem(vocab, 2)

    def at_y(by):
        return x_lo * 8 + lax.rem(y + by + 4, 4) * 2 + core

    def along_z(by):
        return lax.rem(z + by + NZ, NZ)

    sibling = (ctx + 1 - 2 * core, vocab)
    y_peer = {by: (at_y(by), vocab) for by in (-1, 1, 2)}
    lo_peer = (lax.rem(ctx + 8, 16), vocab)
    chip_peer = {
        (lo, by): (lax.rem(x_lo + lo, 2) * 8 + lax.rem(y + by + 4, 4) * 2 + core, vocab)
        for lo, by in CHIPS
    }
    cut_peer = (lax.rem(ctx + 8, 16), z * 2 + 1 - x_hi)
    hi_peer = (ctx, z * 2 + 1 - x_hi)
    z_peer = {by: (ctx, along_z(by) * 2 + x_hi) for by in (-3, -2, -1, 1, 2, 3, 4)}

    barrier = pltpu.get_barrier_semaphore()
    peers = [sibling, cut_peer, hi_peer, *chip_peer.values(), *z_peer.values()]
    for peer in peers:
        pl.semaphore_signal(barrier, inc=1, device_id=peer, device_id_type=MESH)

    def load(index, src, dst):
        copy = pltpu.make_async_copy(src, dst, local_sem.at[index])
        copy.start()
        return copy

    small = [
        load(0, ld_hbm, ld_ref), load(1, seg_hbm, seg_ref), load(2, tgt_hbm, tgt_ref),
        load(3, k_hbm, k_ref), load(4, v_hbm, v_ref),
    ]
    load_q = load(5, q_hbm, q_ref)

    arrivals = {}

    def move(group, key, src, dst, peer):
        index = arrivals.setdefault(key, len(arrivals))
        pltpu.make_async_remote_copy(
            src_ref=src, dst_ref=dst, send_sem=send_sem.at[GROUPS.index(group)],
            recv_sem=recv_sem.at[index], device_id=peer, device_id_type=MESH,
        ).start()

    def arrived(like, *key):
        pltpu.make_async_copy(like, like, recv_sem.at[arrivals[key]]).wait()

    def departed(like, group):
        pltpu.make_async_copy(like, like, send_sem.at[GROUPS.index(group)]).wait()

    def strip(at_lo, at_row, of_core):
        return of_core * 8 + at_lo * 4 + at_row

    def item(lo, by, first=0, count=NZ):
        row = lax.rem(y + by + 4, 4)
        return wo.at[pl.ds(first, count), strip(lax.rem(x_lo + lo, 2), row, core)]

    own_strip = strip(x_lo, y, core)

    def pass_item(key, lo, by, peer, first=0, count=NZ):
        view = item(lo, by, first, count)
        move("wo", key, view, view, peer)

    def wo_0():
        rows = pl.ds(pl.multiple_of(own_strip * 16, 16), 16)
        for by in OTHERS:
            cols = pl.ds(pl.multiple_of(along_z(by) * DZ, 128), DZ)
            move("strip", ("z",), wo_ref.at[rows, cols], wo.at[z, own_strip], z_peer[by])
        cols = pl.ds(pl.multiple_of(z * DZ, 128), DZ)
        return load(6, wo_ref.at[rows, cols], wo.at[z, own_strip])

    one_item = wo.at[0, pl.ds(0, 8)]

    def to_core(lo, by):
        view = item(lo, by)
        move("strip" if (lo, by) == (0, 0) else "wo", ("core",), view, view, sibling)

    def wo_1():
        arrived(wo.at[0, pl.ds(0, NZ - 1)], "z")
        own_strip_copy.wait()
        pass_item(("up",), 0, 0, y_peer[1])
        pass_item(("down",), 0, 0, y_peer[-1])
        pass_item(("lo",), 0, 0, lo_peer)
        to_core(0, 0)

    def wo_2():
        arrived(one_item, "up")
        pass_item(("far",), 0, -1, y_peer[1], 0, 4)
        pass_item(("lo_up",), 0, -1, lo_peer, 0, 4)
        to_core(0, -1)
        arrived(one_item, "down")
        pass_item(("far",), 0, 1, y_peer[-1], 4, 4)
        pass_item(("lo_down",), 0, 1, lo_peer, 0, 4)
        to_core(0, 1)

    def wo_3():
        arrived(one_item, "lo")
        pass_item(("lo_up",), 1, 0, y_peer[1], 4, 4)
        pass_item(("lo_down",), 1, 0, y_peer[-1], 4, 4)
        to_core(1, 0)

    def wo_4():
        arrived(one_item, "far")
        pass_item(("lo_far",), 0, 2, lo_peer, 0, 4)
        to_core(0, 2)
        arrived(one_item, "lo_up")
        pass_item(("lo_far",), 1, -1, y_peer[1], 4, 2)
        to_core(1, -1)
        arrived(one_item, "lo_down")
        pass_item(("lo_far",), 1, 1, y_peer[-1], 6, 2)
        to_core(1, 1)

    def wo_5():
        arrived(one_item, "lo_far")
        to_core(1, 2)

    def wo_6():
        arrived(wo.at[pl.ds(0, 4)], "core")

    def part_rows(piece):
        return WH_ROWS // (8 if KINDS[piece] == "Y" else 4)

    def part_start(piece, by):
        if KINDS[piece] == "Y":
            index = lax.rem(y + by + 4, 4) * 2 + core
        else:
            index = lax.rem(x_lo + by, 2) * 2 + core
        return index * part_rows(piece) + piece * WH_ROWS

    def piece_view(piece, by, low=0, size=None):
        size = part_rows(piece) if size is None else size
        return wh.at[pl.ds(pl.multiple_of(part_start(piece, by) + low, 16), size), pl.ds(NV, NV)]

    def wh_rows(count):
        return wh.at[pl.ds(0, count), pl.ds(0, NV)]

    def fetch_0(piece):
        by = 0 if KINDS[piece] == "Y" else 1
        rows = pl.ds(pl.multiple_of(part_start(piece, by), 16), part_rows(piece))
        move("wh", ("cut", piece), wh_ref.at[rows, :], piece_view(piece, by), cut_peer)

    def pass_part(key, view, peer):
        move("wh", key, view, view, peer)

    def fetch_1(piece):
        arrived(wh_rows(part_rows(piece)), "cut", piece)
        view = piece_view(piece, 0)
        if KINDS[piece] == "Y":
            pass_part(("next", piece), view, y_peer[1])
            pass_part(("next", piece), view, y_peer[-1])
        else:
            pass_part(("next", piece), view, lo_peer)
        pass_part(("wh_core",), view, sibling)

    def fetch_2(piece):
        size = part_rows(piece)
        if KINDS[piece] == "X":
            arrived(wh_rows(size), "next", piece)
            pass_part(("wh_core",), piece_view(piece, 1), sibling)
            return
        half = size // 2
        arrived(wh_rows(2 * size), "next", piece)
        pass_part(("second", piece), piece_view(piece, -1, 0, half), y_peer[1])
        pass_part(("second", piece), piece_view(piece, 1, half, half), y_peer[-1])
        pass_part(("wh_core",), piece_view(piece, -1), sibling)
        pass_part(("wh_core",), piece_view(piece, 1), sibling)

    def fetch_3(piece):
        arrived(wh_rows(part_rows(piece)), "second", piece)
        pass_part(("wh_core",), piece_view(piece, 2), sibling)

    def fetch_4():
        arrived(wh_rows(WH_ROWS // 2 * len(KINDS)), "wh_core")

    for copy in small:
        copy.wait()

    lane = lax.broadcasted_iota(jnp.int32, (8, TOK), 1)
    running = jnp.concatenate([ld_ref[...], jnp.zeros((6, TOK), F32)], axis=0)
    shift = 1
    while shift < TOK:
        running = running + jnp.where(lane >= shift, pltpu.roll(running, shift, axis=1), 0.0)
        shift *= 2
    seg_row = seg_ref[...].astype(F32)
    table = jnp.concatenate(
        [running[0:2], seg_row, tgt_ref[...].astype(F32), jnp.zeros((124, TOK), F32)], axis=0
    )
    columns[...] = table.T
    seg_col = columns[:, 2:3]
    seg_last = seg_col[TOK - 1 : TOK, :]

    decay = []
    own_state = []
    for h in range(2):
        head = slice(h * HD, (h + 1) * HD)
        cum_col = columns[:, h : h + 1]
        last = cum_col[TOK - 1 : TOK, :]
        tail = jnp.where(seg_col == seg_last, jnp.exp(last - cum_col), 0.0)
        weighted = (k_ref[:, head].astype(F32) * tail).astype(BF16)
        summary = lax.dot_general(
            weighted, v_ref[:, head], (((0,), (0,)), ((), ())), preferred_element_type=F32
        )
        own_state.append(summary)
        decay.append(jnp.exp(last))

    def pack(start, state, falloff, seg):
        state_out[start : start + HD, :] = state.astype(BF16)
        row = lax.broadcasted_iota(jnp.int32, (16, HD), 0)
        high = falloff.astype(BF16).astype(F32)
        block = jnp.where(row == 0, high, jnp.where(row == 1, falloff - high, 0.0))
        block = jnp.where(row == 2, seg, block)
        state_out[start + HD : start + STATE, :] = block.astype(BF16)

    def unpack(start):
        block = state_in[start + HD : start + STATE, :].astype(F32)
        return (
            state_in[start : start + HD, :].astype(F32),
            block[0:1, 0:1] + block[1:2, 0:1],
            block[2:3, 0:1],
        )

    def join(first, second):
        state = jnp.where(first[2] == second[2], second[1], 0.0) * first[0] + second[0]
        return state, first[1] * second[1], second[2]

    def choose(flag, a, b):
        return tuple(jnp.where(flag, one, other) for one, other in zip(a, b))

    def of_head(h):
        return own_state[h], decay[h], seg_last

    pack(0, *choose(core == 0, of_head(1), of_head(0)))
    def send_res(offsets):
        for by in offsets:
            cols = pl.ds(pl.multiple_of(along_z(by) * DZ, 128), DZ)
            move("res", ("res",), res_hbm.at[:, cols], res.at[z], z_peer[by])

    pl.semaphore_wait(barrier, len(peers))
    rows = pl.ds(0, STATE)
    move("state", ("state_core",), state_out.at[rows], state_in.at[rows], sibling)
    own_strip_copy = wo_0()
    send_res(OTHERS[:EARLY])
    for piece in range(len(KINDS)):
        fetch_0(piece)
    cols = pl.ds(pl.multiple_of(z * DZ, 128), DZ)
    own_res = load(7, res_hbm.at[:, cols], res.at[z])
    load_gain = load(8, gain_hbm.at[:, cols], gain_ref)

    def inside(h):
        head = slice(h * HD, (h + 1) * HD)
        cum_col = columns[:, h : h + 1]
        cum_row = running[h : h + 1, :]
        for low in (0, 256):
            high = low + 256
            scores = lax.dot_general(
                q_ref[low:high, head], k_ref[0:high, head], (((1,), (1,)), ((), ())),
                preferred_element_type=F32,
            )
            at_row = lax.broadcasted_iota(jnp.int32, (256, high), 0) + low
            at_col = lax.broadcasted_iota(jnp.int32, (256, high), 1)
            allowed = (at_row >= at_col) & (seg_col[low:high] == seg_row[:, 0:high])
            spread = cum_col[low:high] - cum_row[:, 0:high]
            weights = jnp.exp(jnp.where(allowed, spread, -1e30))
            mixing = (scores * weights).astype(BF16)
            within[h, low:high, :] = dot(mixing, v_ref[0:high, head])

    arrived(state_in.at[pl.ds(0, STATE)], "state_core")
    own_wh = load(9, wh_ref, wh.at[:, pl.ds(0, NV)])
    own = choose(core == 0, of_head(0), of_head(1))
    other = unpack(0)
    first = choose(core == 0, own, other)
    second = choose(core == 0, other, own)
    chip = join(first, second)
    pack(STATE, *chip)
    for index, peer in enumerate(CHIPS):
        src = state_out.at[pl.ds(STATE, STATE)]
        dst = state_in.at[pl.ds((1 + index) * STATE, STATE)]
        move("state", ("chips",), src, dst, chip_peer[peer])
    load_q.wait()
    inside(0)
    inside(1)
    arrived(state_in.at[pl.ds(STATE, len(CHIPS) * STATE)], "chips")
    chips = {(0, 0): chip}
    for index, (lo, by) in enumerate(CHIPS):
        chips[lo, by if by in (0, 2) else -by] = unpack((1 + index) * STATE)

    def chip_at(target):
        picked = chip
        for (lo, by), value in chips.items():
            if (lo, by) != (0, 0):
                number = lax.rem(x_lo + lo, 2) * 4 + lax.rem(y + by + 4, 4)
                picked = choose(number == target, value, picked)
        return picked

    my_chip = x_lo * 4 + y
    total = chip_at(0)
    before = choose(my_chip == 0, (jnp.zeros((HD, HD), F32),) + chip[1:], total)
    for target in range(1, 7):
        total = join(total, chip_at(target))
        before = choose(my_chip > target, total, before)
    inner = choose(my_chip == 0, first, join(before, first))
    mine = choose(core == 0, before, inner)
    others = choose(core == 0, inner, before)
    prior = mine[2]
    state_out[2 * STATE : 2 * STATE + HD, :] = others[0].astype(BF16)
    last_rows = pl.ds(8 * STATE, HD)
    move(
        "state", ("incoming",), state_out.at[pl.ds(2 * STATE, HD)], state_in.at[last_rows], sibling
    )
    wo_1()
    arrived(state_in.at[last_rows], "incoming")
    received = state_in[8 * STATE : 8 * STATE + HD, :].astype(F32)
    incoming = [jnp.where(core == h, mine[0], received).astype(BF16) for h in range(2)]

    def own_heads(sub):
        return attn.at[x_hi if sub % 2 else 1 - x_hi, pl.ds(sub // 2 * 128, 128)]

    def wait_heads(step, key):
        arrived(heads.at[0, pl.ds(0, 2)], "heads", step, key)

    def send_heads(way, step, sub, key):
        src = own_heads(sub) if step == 0 else heads.at[GATHER_FROM[way][step], sub]
        dst = heads.at[GATHER_TO[way][step], sub]
        move("heads", ("heads", step, key), src, dst, z_peer[1 if way == 0 else -1])

    def gather_heads(step, sub):
        if step > 0:
            wait_heads(step - 1, sub)
        for way in range(2):
            send_heads(way, step, sub, sub)

    def last_heads(wave):
        for way in range(2):
            wait_heads(2, 2 * wave + way)
            send_heads(way, 3, 2 * wave + way, wave)

    for h in range(2):
        head = slice(h * HD, (h + 1) * HD)
        scale = jnp.where(seg_col == prior, jnp.exp(columns[:, h : h + 1]), 0.0)
        carried = dot(q_ref[:, head], incoming[h])
        output = within[h] + scale * carried
        mean = jnp.mean(output * output, axis=-1, keepdims=True)
        scaled = (output * lax.rsqrt(mean + EPSILON)).astype(BF16)
        for j in range(NZ):
            for half in range(2):
                low = (2 * j + half) * CH
                attn[half, j * CH : (j + 1) * CH, head] = scaled[low : low + CH]
    for sub in range(2):
        gather_heads(0, sub)
    gather_heads(1, 0)
    gather_heads(1, 1)
    gather_heads(0, 2)
    wo_2()
    wo_3()
    for j in range(NZ):
        rows = pl.ds(pl.multiple_of((2 * j + x_hi) * CH, CH), CH)
        goals[j * CH : (j + 1) * CH, :] = columns[rows, :]
    gather_heads(2, 0)
    gather_heads(0, 3)
    gather_heads(2, 1)
    gather_heads(1, 2)
    wo_4()
    fetch_1(0)
    gather_heads(1, 3)
    last_heads(0)
    wo_5()
    gather_heads(2, 2)
    fetch_1(1)
    fetch_1(2)
    wo_6()

    def project(slot, wave):
        if slot == 0:
            left = jnp.concatenate([own_heads(2 * wave + i)[...] for i in range(2)], axis=0)
        else:
            left = heads[slot, 2 * wave : 2 * wave + 2].reshape(HALF, HALF)
        return dot(left, wo[along_z(SLOT_OFFSET[slot])].reshape(HALF, DZ))

    def accumulate(wave, *slots):
        value = partial[wave]
        for slot in slots:
            value = value + project(slot, wave)
        partial[wave] = value

    def swap(wave):
        total = partial[wave] + project(7, wave)
        for i in range(2):
            sub = 2 * wave + i
            swap_out[sub * 64 : sub * 64 + 64, :] = total[i * 64 : i * 64 + 64].astype(BF16)
            view = pl.ds(sub * 64, 64)
            move("swap", ("swap", sub), swap_out.at[view], swap_in.at[view], hi_peer)
        hidden[wave * 128 : wave * 128 + 128, :] = total[128:]

    partial[0] = project(0, 0) + project(1, 0) + project(2, 0)
    accumulate(0, 3, 4)
    accumulate(0, 5, 6)
    gather_heads(2, 3)
    wait_heads(3, 0)
    swap(0)
    send_res(OTHERS[EARLY:])
    partial[1] = project(0, 1) + project(1, 1) + project(2, 1)
    last_heads(1)
    fetch_1(3)
    fetch_1(4)
    fetch_1(5)
    accumulate(1, 3, 4)

    def sub_rows(sub):
        return pl.ds(sub * 64, 64)

    def wait_hidden(step, key):
        arrived(slices.at[0, pl.ds(0, 128)], "hidden", step, key)

    def send_hidden(way, step, sub, key):
        src = slices.at[GATHER_FROM[way][step], sub_rows(sub)]
        dst = slices.at[GATHER_TO[way][step], sub_rows(sub)]
        move("hidden", ("hidden", step, key), src, dst, z_peer[1 if way == 0 else -1])

    def gather_hidden(step, sub):
        if step > 0:
            wait_hidden(step - 1, sub)
        for way in range(2):
            send_hidden(way, step, sub, sub)

    def last_hidden(wave):
        for way in range(2):
            wait_hidden(2, 2 * wave + way)
            send_hidden(way, 3, 2 * wave + way, wave)

    def finish(sub):
        arrived(swap_in.at[pl.ds(0, 64)], "swap", sub)
        rows = slice(sub * 64, (sub + 1) * 64)
        value = hidden[rows, :] + swap_in[rows, :].astype(F32)
        value = value + res[2 * sub : 2 * sub + 2].reshape(64, DZ).astype(F32)
        hidden[rows, :] = value
        slices[0, rows, :] = (value * gain_ref[...]).astype(BF16)
        gather_hidden(0, sub)

    own_tiles = (slice(0, 256), slice(256, 512), slice(512, 640))
    other_tiles = (slice(640, 896), slice(896, 1152), slice(1152, 1280))
    all_tiles = tuple(slice(i * TILE, (i + 1) * TILE) for i in range(5))

    def multiply(slots, low, high, cols, more=True):
        value = logits[low:high, cols] if more else 0.0
        for slot in slots:
            deep = pl.ds(pl.multiple_of(along_z(SLOT_OFFSET[slot]) * DZ, DZ), DZ)
            value = value + dot(slices[slot, low:high, :], wh[deep, cols])
        logits[low:high, cols] = value

    own_res.wait()
    load_gain.wait()
    arrived(res.at[pl.ds(0, NZ - 1)], "res")
    finish(0)
    finish(1)
    accumulate(1, 5, 6)
    wait_heads(3, 1)
    swap(1)
    gather_hidden(1, 0)
    finish(2)
    gather_hidden(1, 1)
    finish(3)
    square = jnp.sum(hidden[...] * hidden[...], axis=1, keepdims=True)
    turned = jnp.broadcast_to(square, (HALF, HD)).T
    squares[0] = jnp.concatenate(
        [turned[0:1, 0:HD], turned[0:1, HD:HALF], jnp.zeros((6, HD), F32)], axis=0
    )
    for slot in range(1, NZ):
        offset = SLOT_OFFSET[slot]
        peer = z_peer[offset if slot == NZ - 1 else -offset]
        move("square", ("square",), squares.at[0], squares.at[slot], peer)

    own_offset = vocab * NV
    other_offset = (z * 2 + 1 - x_hi) * NV

    def summarize(low, high):
        size = high - low
        values = logits[low:high, :] * factor[low:high]
        top = jnp.max(values, axis=1, keepdims=True)
        mass = jnp.sum(jnp.exp(values - top), axis=1, keepdims=True)
        column = lax.broadcasted_iota(jnp.int32, (size, 2 * NV), 1)
        column = jnp.where(column < NV, column + own_offset, column - NV + other_offset)
        goal = goals[low:high, 3:4].astype(jnp.int32)
        hit = jnp.sum(jnp.where(column == goal, values, 0.0), axis=1, keepdims=True)
        lane_of = lax.broadcasted_iota(jnp.int32, (size, HD), 1)
        stats[low:high, :] = jnp.where(lane_of == 0, top, jnp.where(lane_of == 1, mass, hit))

    own_wh.wait()
    fetch_2(0)
    for tile in own_tiles:
        multiply((0,), 0, HALF, tile, False)
    gather_hidden(1, 2)
    fetch_2(1)
    fetch_2(2)
    gather_hidden(1, 3)
    fetch_2(3)
    for tile in own_tiles:
        multiply((1, 2), 0, HALF, tile)
    gather_hidden(2, 0)
    fetch_2(4)
    gather_hidden(2, 1)
    fetch_2(5)
    gather_hidden(2, 2)
    fetch_3(1)
    fetch_3(2)
    fetch_3(3)
    gather_hidden(2, 3)
    fetch_3(4)
    fetch_3(5)
    for tile in own_tiles:
        multiply((3, 4), 0, HALF, tile)
    last_hidden(0)
    last_hidden(1)
    fetch_4()
    for tile in other_tiles:
        multiply((0, 1, 2, 3, 4), 0, HALF, tile, False)
    total_square = squares[0]
    arrived(squares.at[pl.ds(0, NZ - 1)], "square")
    for slot in range(1, NZ):
        total_square = total_square + squares[slot]
    factor = lax.rsqrt(total_square / D + EPSILON)
    factor = jnp.concatenate([factor, jnp.zeros((HD - 8, HD), F32)], axis=0).T
    factor = jnp.concatenate([factor[:, 0:1], factor[:, 1:2]], axis=0)
    for tile in all_tiles:
        multiply((5, 6), 0, HALF, tile)
    for i in range(2):
        wait_hidden(3, i)
        for tile in all_tiles:
            multiply((7,), i * 128, i * 128 + 128, tile)
        summarize(i * 128, i * 128 + 128)
    turned = stats[...].T
    for half in range(2):
        stats_out[half] = turned[0:8, half * HD : (half + 1) * HD]
    for by in (4, 3, -3, 2, -2, 1, -1):
        move("stats", ("stats",), stats_out.at[along_z(by) // 4], stats_in.at[by + 3], z_peer[by])
    blocks = [stats_out[z // 4]]
    arrived(stats_in.at[pl.ds(0, NZ - 1)], "stats")
    for by in OTHERS:
        blocks.append(stats_in[by + 3])
    top = blocks[0][0:1]
    for block in blocks[1:]:
        top = jnp.maximum(top, block[0:1])
    mass = jnp.zeros((1, HD), F32)
    hit = jnp.zeros((1, HD), F32)
    for block in blocks:
        mass = mass + block[1:2] * jnp.exp(block[0:1] - top)
        hit = hit + block[2:3]
    result = hit - top - jnp.log(mass)
    quarter = lax.rem(z, 4)
    picked = result[:, 0:CH]
    for i in range(1, 4):
        picked = jnp.where(quarter == i, result[:, i * CH : (i + 1) * CH], picked)
    out_ref[...] = picked
    departed(state_in, "state")
    departed(res.at[pl.ds(0, NZ - 1)], "res")
    departed(wo.at[0, pl.ds(0, 15)], "strip")
    departed(wo.at[pl.ds(0, NZ - 1)], "wo")
    departed(wh_rows(D), "wh")
    departed(heads.at[pl.ds(0, NZ - 1)], "heads")
    departed(swap_out, "swap")
    departed(slices.at[pl.ds(0, NZ - 1)], "hidden")
    departed(squares.at[pl.ds(0, NZ - 1)], "square")
    departed(stats_in.at[pl.ds(0, NZ - 1)], "stats")


def shards(
    query_rows, key_rows, value_rows, log_decay, segment_ids, residual, out_weight, final_gain,
    head_weight, targets,
):
    vmem = pl.BlockSpec(memory_space=pltpu.VMEM)
    hbm = pl.BlockSpec(memory_space=pl.ANY)
    dma = pltpu.SemaphoreType.DMA
    result = pl.pallas_call(
        kernel,
        out_shape=jax.ShapeDtypeStruct((1, CH), F32),
        in_specs=[hbm] * 10,
        out_specs=vmem,
        scratch_shapes=[
            pltpu.VMEM((TOK, 2 * HD), BF16),
            pltpu.VMEM((TOK, 2 * HD), BF16),
            pltpu.VMEM((TOK, 2 * HD), BF16),
            pltpu.VMEM((2, TOK), F32),
            pltpu.VMEM((1, TOK), jnp.int32),
            pltpu.VMEM((1, TOK), jnp.int32),
            pltpu.VMEM((NZ, CH, DZ), BF16),
            pltpu.VMEM((1, DZ), F32),
            pltpu.VMEM((NZ, 16, 16, DZ), BF16),
            pltpu.VMEM((D, 2 * NV), BF16),
            pltpu.VMEM((2, HALF, 2 * HD), BF16),
            pltpu.VMEM((NZ, 4, 128, 2 * HD), BF16),
            pltpu.VMEM((2, HALF, DZ), F32),
            pltpu.VMEM((HALF, DZ), F32),
            pltpu.VMEM((HALF, DZ), BF16),
            pltpu.VMEM((HALF, DZ), BF16),
            pltpu.VMEM((NZ, HALF, DZ), BF16),
            pltpu.VMEM((HALF, 2 * NV), F32),
            pltpu.VMEM((NZ, 8, HD), F32),
            pltpu.VMEM((2, TOK, HD), F32),
            pltpu.VMEM((TOK, HD), F32),
            pltpu.VMEM((HALF, HD), F32),
            pltpu.VMEM((2 * STATE + HD, HD), BF16),
            pltpu.VMEM((8 * STATE + HD, HD), BF16),
            pltpu.VMEM((HALF, HD), F32),
            pltpu.VMEM((2, 8, HD), F32),
            pltpu.VMEM((NZ, 8, HD), F32),
            dma((10,)),
            dma((len(GROUPS),)),
            dma((ARRIVALS,)),
        ],
        compiler_params=pltpu.CompilerParams(
            collective_id=0, has_side_effects=True, vmem_limit_bytes=56 * 1024 * 1024
        ),
        name="layer",
    )(
        query_rows, key_rows, value_rows, log_decay, segment_ids.reshape(1, -1),
        targets.reshape(1, -1), residual, final_gain.reshape(1, -1), out_weight, head_weight,
    )
    return result.reshape(CH)


def solution(mesh):
    in_specs = (
        P("ctx", "vocab"),
        P("ctx", "vocab"),
        P("ctx", "vocab"),
        P("vocab", "ctx"),
        P("ctx"),
        P(("ctx", "vocab"), None),
        P("vocab", None),
        P(),
        P(None, "vocab"),
        P("ctx"),
    )
    out_specs = P(("ctx", "vocab"))
    return jax.shard_map(shards, mesh=mesh, in_specs=in_specs, out_specs=out_specs, check_vma=False)
```
